32 devices in a mesh: grp: 2 (over y), tile: 8 (over z, x), mode: 2 (over core).
Axes of the slice: x: 2, y: 2, z: 4, core: 2. Of those that a mesh axis runs over, the one named last changes fastest.
Arguments:
- object_slab: float32 [2048, 2, 256], P(('grp', 'tile')), parts along dimension 0, may hold values from -6 to 6
- probe_modes: float32 [16, 128, 256], P(('grp', 'mode')), parts along dimension 0, may hold values from -1.2 to 1.2
- frames: float32 [64, 128, 128], P(('grp', 'tile')), parts along dimension 0, may hold values from 0.1 to 10
- offsets: int32 [64, 2], P(('grp', 'tile')), parts along dimension 0, may hold values from 0 to 128, as said below
- counts: int32 [16], P(('grp', 'tile')), parts along dimension 0, may hold values from 0 to 4, as said below
Outputs:
- updated_object: float32 [2048, 2, 256], P(('grp', 'tile')), parts along dimension 0
- probe_direction: float32 [16, 128, 256], P(('grp', 'mode')), parts along dimension 0
The draws below stay inside these ranges and needn't reach their ends.
There are 2 independent parts, one for each index of `grp`. The reference program is written for one: setup_inputs(seed, part) draws one part's arguments, and reference() takes and returns one part's arrays. A program takes and returns all parts, laid end to end along the dimension named above; each array names one. Nothing has to cross between parts.
Inputs may be any that keep to these rules, and one draw needn't show every extreme that they name: `offsets`: rows lie in 0 to 127, columns in 0 to 128. For every tile t below 4, counts[t] + counts[t + 4] <= 4; some tile holds 4 live positions.
All inputs are finite; a program needn't handle non-finite values.
Results may differ from the reference program's by a relative error of at most 0.0068.
Values sent between devices are 32-bit elements; how exact they have to be, the bound alone decides.
A program may use at most 64 MiB of HBM per device.

```python
import math
import jax
import jax.numpy as jnp
from jax import lax

FRAME = 128
MODES = 8
R_DEV = 128
W = 256
P_CAP = 4
TILES = 8
NROWS = 1024
POS = 32


def draw_offsets(key, part):
    key = jax.random.fold_in(key, 23)
    row_key, col_key = jax.random.split(key, 2)
    row_offsets = jax.random.randint(row_key, (POS,), 0, R_DEV)
    col_offsets = jax.random.randint(col_key, (POS,), 0, W - FRAME + 1)
    row_offsets = row_offsets.at[0].set(R_DEV - 1)
    col_offsets = col_offsets.at[0].set(0)
    col_offsets = col_offsets.at[1].set(W - FRAME)
    return jnp.stack([row_offsets, col_offsets], 1).astype(jnp.int32)


def draw_counts(key, part):
    key = jax.random.fold_in(key, 11)
    subkeys = jax.random.split(key, 4)
    half_tiles = TILES // 2
    first_loads = jax.random.randint(subkeys[0], (half_tiles,), 0, P_CAP + 1)
    extra_gap = jax.random.randint(subkeys[1], (half_tiles,), 0, P_CAP // 4 + 1)
    full_at = jax.random.randint(subkeys[2], (), 0, half_tiles)
    first_loads = jnp.where(jnp.arange(half_tiles) == full_at, P_CAP, first_loads)
    second_loads = jnp.maximum(P_CAP - first_loads - extra_gap, 0)
    flipped = jax.random.randint(subkeys[3], (half_tiles,), 0, 2) == 1
    lower_loads = jnp.where(flipped, second_loads, first_loads)
    upper_loads = jnp.where(flipped, first_loads, second_loads)
    return jnp.concatenate([lower_loads, upper_loads]).astype(jnp.int32)


def level_of(own_key, dims, cuts, low, top_value):
    gain, own = 1.0, jax.random.fold_in(own_key, 6)
    for axis_at, shards_of in cuts:
        heights = jnp.exp(jax.random.uniform(jax.random.fold_in(own, axis_at), (shards_of,), jnp.float32, low / len(cuts), top_value / len(cuts)))
        gain = gain * jnp.repeat(heights, dims[axis_at] // shards_of).reshape([-1 if axis == axis_at else 1 for axis in range(len(dims))])
    return gain


def normal_values(rng, dims, width, bound, pieces=(), held_as=jnp.bfloat16):
    loudness = level_of(rng, dims, pieces, -0.22, 0.18) if pieces else 1.0
    drawn = jax.random.normal(rng, dims, jnp.float32) * width * loudness
    return jnp.minimum(jnp.maximum(drawn, -bound), bound).astype(held_as)


def setup_inputs(seed: int = 0, part: int = 0) -> dict:
    arg_keys = jax.random.split(jax.random.key(seed), 6)
    part_keys = jax.random.split(jax.random.fold_in(arg_keys[5], part), 6)
    return {
        "object_slab": normal_values(part_keys[0], (NROWS, 2, W), 1.0, 6.0, ((0, 8),), jnp.float32),
        "probe_modes": normal_values(part_keys[1], (MODES, FRAME, 2 * FRAME), 0.2, 1.2, ((0, 2),), jnp.float32),
        "frames": jnp.clip(jnp.exp(math.log(10.0) - 4.6051702 * jax.random.uniform(part_keys[2], (POS, FRAME, FRAME), jnp.float32) ** level_of(part_keys[2], (POS, FRAME, FRAME), ((0, 8),), -0.2, 0.2)), 0.1, 10.0),
        "offsets": draw_offsets(jax.random.fold_in(jax.random.fold_in(arg_keys[5], part), 71), part),
        "counts": draw_counts(jax.random.fold_in(jax.random.fold_in(arg_keys[5], part), 71), part),
    }


def dft_tables():
    indices = jnp.arange(FRAME, dtype=jnp.int32)
    phases = (indices[:, None] * indices[None, :] % FRAME).astype(jnp.float32) * (2.0 * jnp.pi / FRAME)
    norm_scale = 1.0 / jnp.sqrt(jnp.float32(FRAME))
    cos_part = (jnp.cos(phases) * norm_scale).astype(jnp.bfloat16)
    sin_part = (-jnp.sin(phases) * norm_scale).astype(jnp.bfloat16)
    right_fwd = jnp.concatenate([jnp.concatenate([cos_part, sin_part], 1), jnp.concatenate([-sin_part, cos_part], 1)], 0)
    right_inv = jnp.concatenate([jnp.concatenate([cos_part, -sin_part], 1), jnp.concatenate([sin_part, cos_part], 1)], 0)
    return (cos_part, sin_part, right_fwd, right_inv)

def rotate_half(values):
    middle = values.shape[-1] // 2
    return jnp.concatenate([-values[..., middle:], values[..., :middle]], -1)

def complex_product(left, right):
    middle = left.shape[-1] // 2
    lre, lim = (left[..., :middle], left[..., middle:])
    rre, rim = (right[..., :middle], right[..., middle:])
    return jnp.concatenate([lre * rre - lim * rim, lre * rim + lim * rre], -1)

def conjugate_product(left, right):
    middle = left.shape[-1] // 2
    lre, lim = (left[..., :middle], left[..., middle:])
    rre, rim = (right[..., :middle], right[..., middle:])
    return jnp.concatenate([lre * rre + lim * rim, lre * rim - lim * rre], -1)

def transform(values, right_table, cos_part, sin_part, sign):
    high = lax.Precision.HIGHEST
    first = jnp.einsum('nmrc,cd->nmrd', values.astype(jnp.float32), right_table.astype(jnp.float32), precision=high)
    first = first.astype(jnp.bfloat16).astype(jnp.float32)
    real_left = jnp.einsum('jr,nmrd->nmjd', cos_part.astype(jnp.float32), first, precision=high)
    imag_left = jnp.einsum('jr,nmrd->nmjd', sin_part.astype(jnp.float32), first, precision=high)
    return real_left + sign * rotate_half(imag_left)

def reference(object_slab, probe_modes, frames, offsets, counts):
    cos_part, sin_part, right_fwd, right_inv = dft_tables()
    padded = jnp.concatenate([object_slab, jnp.zeros((FRAME, 2, W), jnp.float32)], 0)
    probe_power = lax.optimization_barrier(jnp.sum(probe_modes[..., :FRAME] ** 2 + probe_modes[..., FRAME:] ** 2, 0))
    zero_index = jnp.int32(0)

    def tile_step(carry, inputs):
        grad_pad, illum_pad, probe_sum = carry
        tile_id, tile_frames, tile_offsets, live_count = inputs
        row_start = (tile_id * R_DEV + tile_offsets[:, 0]).astype(jnp.int32)
        col_start = tile_offsets[:, 1].astype(jnp.int32)
        live_mask = jnp.arange(P_CAP, dtype=jnp.int32) < live_count

        def cut_patch(row_at, col_at):
            return lax.dynamic_slice(padded, (row_at, zero_index, col_at), (FRAME, 2, FRAME))
        patches = jax.vmap(cut_patch)(row_start, col_start).reshape(P_CAP, FRAME, 2 * FRAME)
        patches = patches * live_mask[:, None, None].astype(jnp.float32)
        psi_waves = complex_product(probe_modes[None], patches[:, None]).astype(jnp.bfloat16)
        far_field = transform(psi_waves, right_fwd, cos_part, sin_part, 1.0)
        power = lax.optimization_barrier(jnp.sum(far_field[..., :FRAME] ** 2 + far_field[..., FRAME:] ** 2, 1))
        factor = jnp.sqrt(tile_frames) / jnp.sqrt(power + 1.0) - 1.0
        corrected = (far_field * jnp.concatenate([factor, factor], -1)[:, None]).astype(jnp.bfloat16)
        back_waves = transform(corrected, right_inv, cos_part, sin_part, -1.0)
        grad_patches = lax.optimization_barrier(jnp.sum(conjugate_product(probe_modes[None], back_waves), 1)).reshape(P_CAP, FRAME, 2, FRAME)
        probe_part = lax.optimization_barrier(jnp.sum(conjugate_product(patches[:, None], back_waves), 0))

        def add_patch(slot_id, slabs):
            grad_now, illum_now = slabs
            row_at = row_start[slot_id]
            col_at = col_start[slot_id]
            old_grad = lax.dynamic_slice(grad_now, (row_at, zero_index, col_at), (FRAME, 2, FRAME))
            grad_now = lax.dynamic_update_slice(grad_now, old_grad + grad_patches[slot_id], (row_at, zero_index, col_at))
            old_illum = lax.dynamic_slice(illum_now, (row_at, col_at), (FRAME, FRAME))
            weight = live_mask[slot_id].astype(jnp.float32)
            illum_now = lax.dynamic_update_slice(illum_now, old_illum + probe_power * weight, (row_at, col_at))
            return (grad_now, illum_now)
        grad_pad, illum_pad = lax.fori_loop(0, P_CAP, add_patch, (grad_pad, illum_pad))
        return ((grad_pad, illum_pad, probe_sum + probe_part), None)
    start = (jnp.zeros((NROWS + FRAME, 2, W), jnp.float32), jnp.zeros((NROWS + FRAME, W), jnp.float32), jnp.zeros((MODES, FRAME, 2 * FRAME), jnp.float32))
    tile_ids = jnp.arange(TILES, dtype=jnp.int32)
    inputs = (tile_ids, frames.reshape(TILES, P_CAP, FRAME, FRAME), offsets.reshape(TILES, P_CAP, 2), counts)
    (grad_pad, illum_pad, probe_sum), _ = lax.scan(tile_step, start, inputs)
    gradient = grad_pad[:NROWS]
    illumination = illum_pad[:NROWS]
    peak = jnp.max(illumination)
    updated_object = object_slab + gradient / (illumination[:, None, :] + 0.1 * peak)
    probe_direction = probe_sum / jnp.sqrt(jnp.float32(POS))
    return (updated_object, probe_direction)
```

```python
import functools

import jax
import jax.numpy as jnp
import numpy as np
from jax import lax
from jax.experimental import pallas as pl
from jax.experimental.pallas import tpu as pltpu
from jax.sharding import PartitionSpec as P

FRAME = 128
MIN_ROWS = 8


def dft_matrices():
    indices = np.arange(FRAME)
    phases = (indices[:, None] * indices[None, :] % FRAME) * (2.0 * np.pi / FRAME)
    cos_part = np.cos(phases) / np.sqrt(FRAME)
    sin_part = -np.sin(phases) / np.sqrt(FRAME)
    fwd = np.block([[cos_part, sin_part], [-sin_part, cos_part]])
    inv = np.block([[cos_part, -sin_part], [sin_part, cos_part]])
    return fwd.astype(jnp.bfloat16), inv.astype(jnp.bfloat16)


def stages_of(tiles):
    bits = tiles.bit_length() - 1
    assert tiles == 1 << bits
    stages, at, rows = [], 0, FRAME
    while at < bits:
        radix = 2 if at == 0 or bits - at == 1 else 4
        after = rows // radix if rows // radix >= MIN_ROWS else rows
        stages.append((at, radix, rows, after))
        rows = after
        at += 1 if radix == 2 else 2
    return stages


def tree(values, join):
    while len(values) > 1:
        values = [join(values[i], values[i + 1]) for i in range(0, len(values), 2)]
    return values[0]


def kernel(
    tiles,
    stages,
    obj,
    probe,
    frames,
    offsets,
    counts,
    fwd,
    inv,
    obj_out,
    probe_out,
    ext,
    power_probe,
    ext_split,
    illum,
    illum_in,
    patches,
    far,
    power,
    power_in,
    factor,
    grad,
    grad_in,
    gext,
    spill_in,
    acc,
    peaks,
    halo_sem,
    relay_sem,
    pp_sem,
    illum_sem,
    power_sem,
    grad_sem,
    spill_sem,
    upd_sem,
    *staged,
):
    n_st = len(stages)
    rs_in, pk_in = staged[:n_st], staged[n_st : 2 * n_st]
    rs_sem, ag_sem, pk_sem = (staged[(2 + j) * n_st : (3 + j) * n_st] for j in range(3))
    slots = frames.shape[0]
    modes = probe.shape[0]
    f = FRAME
    me = lax.axis_index("tile")
    core = lax.axis_index("mode")
    other = 1 - core
    has_left, has_right = me > 0, me < tiles - 1
    left, right = jnp.maximum(me - 1, 0), jnp.minimum(me + 1, tiles - 1)

    def remote(src, dst, sems, **where):
        return pltpu.make_async_remote_copy(
            src_ref=src,
            dst_ref=dst,
            send_sem=sems[0],
            recv_sem=sems[1],
            device_id=where,
            device_id_type=pl.DeviceIdType.MESH,
        )

    def pair(sem, *at):
        return (sem.at[(0, *at)], sem.at[(1, *at)])

    own_power = jnp.zeros((f, f), jnp.float32)
    for k in range(modes):
        own_power += probe[k, :, :f] ** 2 + probe[k, :, f:] ** 2
    power_probe[0] = own_power

    barrier = pltpu.get_barrier_semaphore()

    def greet(**where):
        pl.semaphore_signal(
            barrier, inc=1, device_id=where, device_id_type=pl.DeviceIdType.MESH
        )

    greet(mode=other)
    greeted = 1
    for at, radix, _, _ in stages:
        for d in range(1, radix):
            greet(tile=me ^ (d << at))
            greeted += 1

    @pl.when(has_left)
    def _():
        greet(tile=left)

    @pl.when(has_right)
    def _():
        greet(tile=right)

    beside = jnp.minimum(me, 1) + jnp.minimum(tiles - 1 - me, 1)
    pl.semaphore_wait(barrier, greeted + beside)

    halo = remote(obj.at[core], ext.at[core, pl.ds(f, f)], pair(halo_sem), tile=left)

    @pl.when(has_left)
    def _():
        halo.start()

    pp_copy = remote(power_probe.at[0], power_probe.at[1], pair(pp_sem), mode=other)
    pp_copy.start()
    ext[:, :f, :] = obj[...]

    def live(s):
        return jnp.clip(counts[0] - s, 0, 1).astype(jnp.float32)

    def dot(a, b):
        return jnp.dot(a, b, preferred_element_type=jnp.float32)

    def split(x):
        high = x.astype(jnp.bfloat16)
        return high, (x - high.astype(jnp.float32)).astype(jnp.bfloat16)

    def shifts(rows, columns, by):
        i = lax.broadcasted_iota(jnp.int32, (rows, columns), 0)
        j = lax.broadcasted_iota(jnp.int32, (rows, columns), 1)
        apart = j - i if rows < columns else i - j
        return jnp.where(apart == by, 1.0, 0.0).astype(jnp.float32)

    def spread(s, values):
        across = shifts(f, 2 * f, offsets[s, 1]).astype(jnp.bfloat16)
        down = (shifts(2 * f, f, offsets[s, 0]) * live(s)).astype(jnp.bfloat16)
        wide = dot(jnp.concatenate(split(values), 0), across).astype(jnp.bfloat16)
        return dot(jnp.concatenate([down, down], 1), wide)

    pp_copy.wait()
    probe_power = power_probe[0] + power_probe[1]
    illum[...] = jnp.zeros_like(illum)

    def light(s, carry):
        illum[...] += spread(s, probe_power)
        return carry

    lax.fori_loop(0, slots, light, 0)
    illum_copy = remote(illum.at[pl.ds(f, f)], illum_in, pair(illum_sem), tile=right)

    @pl.when(has_right)
    def _():
        illum_copy.start()

    relay = remote(
        ext.at[core, pl.ds(f, f)], ext.at[core, pl.ds(f, f)], pair(relay_sem), mode=other
    )

    @pl.when(has_right)
    def _():
        halo.wait_recv()
        relay.start()
        relay.wait_recv()

    @pl.when(jnp.logical_not(has_right))
    def _():
        ext[:, f:, :] = jnp.zeros((2, f, 2 * f), jnp.float32)

    for part in range(2):
        for j, piece in enumerate(split(ext[part])):
            ext_split[:, (2 * part + j) * 2 * f : (2 * part + j + 1) * 2 * f] = piece

    def window(s):
        down = (shifts(f, 2 * f, offsets[s, 0]) * live(s)).astype(jnp.bfloat16)
        across = shifts(2 * f, f, offsets[s, 1]).astype(jnp.bfloat16)
        rows = dot(down, ext_split[...]).astype(jnp.bfloat16)
        both = jnp.concatenate([rows[:, : 4 * f], rows[:, 4 * f :]], 0)
        return dot(both, jnp.concatenate([across, across], 0))

    def swap(x):
        return jnp.concatenate(
            [
                jnp.concatenate([x[:f, :f], x[f:, :f]], 1),
                jnp.concatenate([x[:f, f:], x[f:, f:]], 1),
            ],
            0,
        )

    def power_copy(s):
        return remote(power.at[s], power_in.at[s], pair(power_sem, s), mode=other)

    def forward(s, carry):
        patch = window(s)
        xr, xi = patch[:f], patch[f:]
        patches[s, :, :f] = xr
        patches[s, :, f:] = xi
        total = jnp.zeros((f, f), jnp.float32)
        for p in range(modes // 2):
            psi = []
            for k in (2 * p, 2 * p + 1):
                pr, pi = probe[k, :, :f], probe[k, :, f:]
                psi.append(
                    jnp.concatenate([pr * xr - pi * xi, pr * xi + pi * xr], 1).astype(jnp.bfloat16)
                )
            half = dot(jnp.concatenate(psi, 0), fwd[...]).astype(jnp.bfloat16)
            wave = dot(inv[...], swap(half))
            far[s, p] = wave
            squares = wave * wave
            total += (squares[:f, :f] + squares[f:, :f]) + (squares[:f, f:] + squares[f:, f:])
        power[s] = total
        power_copy(s).start()
        return carry

    lax.fori_loop(0, slots, forward, 0)

    @pl.when(has_left)
    def _():
        illum_copy.wait_recv()

    @pl.when(jnp.logical_not(has_left))
    def _():
        illum_in[...] = jnp.zeros_like(illum_in)

    @pl.when(has_right)
    def _():
        illum_copy.wait_send()

    illum[:f] = illum[:f] + illum_in[...]
    high = jnp.max(illum[:f].reshape(f // 8, 8, 2 * f), 0)
    peaks[0] = jnp.maximum(high[:, :f], high[:, f:])

    def peak_copies(i):
        at, radix, _, _ = stages[i]
        return [
            remote(
                peaks.at[i], pk_in[i].at[d - 1], pair(pk_sem[i], d - 1), tile=me ^ (d << at)
            )
            for d in range(1, radix)
        ]

    def peak_start(i):
        for copy in peak_copies(i):
            copy.start()

    def peak_finish(i):
        for copy in peak_copies(i):
            copy.wait()
        radix = stages[i][1]
        peaks[i + 1] = tree([peaks[i]] + [pk_in[i][d] for d in range(radix - 1)], jnp.maximum)

    peak_start(0)

    def rescale(s, carry):
        power_copy(s).wait()
        factor[s] = (
            jnp.sqrt(frames[s]) * lax.rsqrt(power[s] + power_in[s] + 1.0) - 1.0
        )
        return carry

    lax.fori_loop(0, slots, rescale, 0)

    starts = [0]
    for at, radix, rows, after in stages:
        digit = lax.rem(me // (1 << at), radix)
        starts.append(starts[-1] + digit * after if after < rows else starts[-1])

    def rows_at(ref, k, start, rows):
        return ref.at[k, pl.ds(pl.multiple_of(start, MIN_ROWS), rows)]

    def rs_copies(i, k):
        at, radix, rows, after = stages[i]
        digit = lax.rem(me // (1 << at), radix)
        copies = []
        for d in range(1, radix):
            start = starts[i] + (digit ^ d) * after if after < rows else starts[i]
            copies.append(
                remote(
                    rows_at(acc, k, start, after),
                    rs_in[i].at[k, d - 1],
                    pair(rs_sem[i], k, d - 1),
                    tile=me ^ (d << at),
                )
            )
        return copies

    def rs_start(i, ks):
        for k in ks:
            for copy in rs_copies(i, k):
                copy.start()

    def rs_finish(i, ks):
        after, radix = stages[i][3], stages[i][1]
        for k in ks:
            for copy in rs_copies(i, k):
                copy.wait()
            here = rows_at(acc, k, starts[i + 1], after)
            here[...] = tree(
                [here[...]] + [rs_in[i][k, d] for d in range(radix - 1)], lax.add
            )

    scale = 1.0 / np.sqrt(np.float32(tiles * slots))

    def finish_sum(ks):
        for k in ks:
            last = stages[-1][3]
            rows_at(probe_out, k, starts[-1], last)[...] = (
                rows_at(acc, k, starts[-1], last)[...] * scale
            )

    def ag_copies(i, k):
        at, radix, rows, after = stages[i]
        if after == rows:
            return []
        here = rows_at(probe_out, k, starts[i + 1], after)
        return [
            remote(here, here, pair(ag_sem[i], k, d - 1), tile=me ^ (d << at))
            for d in range(1, radix)
        ]

    def ag_start(i, ks):
        for k in ks:
            for copy in ag_copies(i, k):
                copy.start()

    def ag_finish(i, ks):
        for k in ks:
            for copy in ag_copies(i, k):
                copy.wait()

    groups = [(2 * p, 2 * p + 1) for p in range(modes // 2)]
    for p, ks in enumerate(groups):
        for k in ks:
            acc[k] = jnp.zeros((f, 2 * f), jnp.float32)

        def backward(s, carry, p=p, ks=ks):
            scaled = factor[s]
            wide = jnp.concatenate([scaled, scaled], 1)
            wide = jnp.concatenate([wide, wide], 0)
            corrected = (far[s, p] * wide).astype(jnp.bfloat16)
            half = dot(swap(corrected), inv[...]).astype(jnp.bfloat16)
            back = dot(fwd[...], swap(half))
            xr, xi = patches[s, :, :f], patches[s, :, f:]
            gr, gi = None, None
            for j, k in enumerate(ks):
                br, bi = back[:f, j * f : (j + 1) * f], back[f:, j * f : (j + 1) * f]
                pr, pi = probe[k, :, :f], probe[k, :, f:]
                r, i = pr * br + pi * bi, pr * bi - pi * br
                gr, gi = (r, i) if gr is None else (gr + r, gi + i)
                acc[k, :, :f] += xr * br + xi * bi
                acc[k, :, f:] += xr * bi - xi * br
            if p == 0:
                grad[0, s], grad[1, s] = gr, gi
            else:
                grad[0, s] += gr
                grad[1, s] += gi
            return carry

        lax.fori_loop(0, slots, backward, 0)
        if p == len(groups) - 1:
            grad_copy = remote(grad.at[other], grad_in, pair(grad_sem), mode=other)
            grad_copy.start()
        rs_start(0, ks)
        if p < n_st:
            peak_finish(p)
            if p + 1 < n_st:
                peak_start(p + 1)

    for i in range(len(groups), n_st):
        peak_finish(i)
        if i + 1 < n_st:
            peak_start(i + 1)

    grad_copy.wait()
    gext[...] = jnp.zeros_like(gext)

    def gather_up(s, carry):
        gext[...] += spread(s, grad[core, s] + grad_in[s])
        return carry

    lax.fori_loop(0, slots, gather_up, 0)
    spill_copy = remote(gext.at[pl.ds(f, f)], spill_in, pair(spill_sem), tile=right)

    @pl.when(has_right)
    def _():
        spill_copy.start()

    for i in range(n_st):
        for ks in groups:
            rs_finish(i, ks)
            if i + 1 < n_st:
                rs_start(i + 1, ks)
            else:
                finish_sum(ks)
                ag_start(i, ks)

    @pl.when(has_left)
    def _():
        spill_copy.wait_recv()

    @pl.when(jnp.logical_not(has_left))
    def _():
        spill_in[...] = jnp.zeros_like(spill_in)

    peak = jnp.max(peaks[n_st])
    obj_out[core] = obj[core] + (gext[:f] + spill_in[...]) / (illum[:f] + 0.1 * peak)
    upd_copy = remote(obj_out.at[core], obj_out.at[core], pair(upd_sem), mode=other)
    upd_copy.start()

    for i in reversed(range(n_st)):
        for ks in groups:
            ag_finish(i, ks)
            if i > 0:
                ag_start(i - 1, ks)

    upd_copy.wait()

    @pl.when(has_left)
    def _():
        halo.wait_send()

    @pl.when(has_right)
    def _():
        relay.wait_send()
        spill_copy.wait_send()


def body(tiles, object_slab, probe_modes, frames, offsets, counts):
    f = FRAME
    stages = stages_of(tiles)
    slots, modes = frames.shape[0], probe_modes.shape[0]
    columns = object_slab.shape[2]
    fwd, inv = dft_matrices()
    f32 = jnp.float32
    vmem = pl.BlockSpec(memory_space=pltpu.VMEM)
    smem = pl.BlockSpec(memory_space=pltpu.SMEM)
    dma = pltpu.SemaphoreType.DMA
    scratch = [
        pltpu.VMEM((2, 2 * f, columns), f32),
        pltpu.VMEM((2, f, f), f32),
        pltpu.VMEM((2 * f, 4 * columns), jnp.bfloat16),
        pltpu.VMEM((2 * f, columns), f32),
        pltpu.VMEM((f, columns), f32),
        pltpu.VMEM((slots, f, 2 * f), f32),
        pltpu.VMEM((slots, modes // 2, 2 * f, 2 * f), f32),
        pltpu.VMEM((slots, f, f), f32),
        pltpu.VMEM((slots, f, f), f32),
        pltpu.VMEM((slots, f, f), f32),
        pltpu.VMEM((2, slots, f, f), f32),
        pltpu.VMEM((slots, f, f), f32),
        pltpu.VMEM((2 * f, columns), f32),
        pltpu.VMEM((f, columns), f32),
        pltpu.VMEM((modes, f, 2 * f), f32),
        pltpu.VMEM((len(stages) + 1, 8, f), f32),
        dma((2,)),
        dma((2,)),
        dma((2,)),
        dma((2,)),
        dma((2, slots)),
        dma((2,)),
        dma((2,)),
        dma((2,)),
    ]
    scratch += [pltpu.VMEM((modes, radix - 1, after, 2 * f), f32) for _, radix, _, after in stages]
    scratch += [pltpu.VMEM((radix - 1, 8, f), f32) for _, radix, _, _ in stages]
    for _ in range(2):
        scratch += [dma((2, modes, radix - 1)) for _, radix, _, _ in stages]
    scratch += [dma((2, radix - 1)) for _, radix, _, _ in stages]
    updated, probe_direction = pl.pallas_call(
        functools.partial(kernel, tiles, stages),
        out_shape=(
            jax.ShapeDtypeStruct((2, f, columns), f32),
            jax.ShapeDtypeStruct((modes, f, 2 * f), f32),
        ),
        in_specs=[vmem, vmem, vmem, smem, smem, vmem, vmem],
        out_specs=(vmem, vmem),
        scratch_shapes=scratch,
        compiler_params=pltpu.CompilerParams(
            collective_id=0, has_side_effects=True, vmem_limit_bytes=40 * 1024 * 1024
        ),
        name="ptycho_step",
    )(object_slab.transpose(1, 0, 2), probe_modes, frames, offsets, counts, fwd, inv)
    return updated.transpose(1, 0, 2), probe_direction


def solution(mesh):
    placed = (
        P(("grp", "tile"), None, None),
        P(("grp", "mode"), None, None),
        P(("grp", "tile"), None, None),
        P(("grp", "tile"), None),
        P(("grp", "tile")),
    )
    return jax.shard_map(
        functools.partial(body, mesh.shape["tile"]),
        mesh=mesh,
        in_specs=placed,
        out_specs=(P(("grp", "tile"), None, None), P(("grp", "mode"), None, None)),
        check_vma=False,
    )
```

```python
import functools

import jax
import jax.numpy as jnp
import numpy as np
from jax import lax
from jax.experimental import pallas as pl
from jax.experimental.pallas import tpu as pltpu
from jax.sharding import PartitionSpec as P

FRAME = 128
MIN_ROWS = 8


def dft_table():
    indices = np.arange(FRAME)
    phases = (indices[:, None] * indices[None, :] % FRAME) * (2.0 * np.pi / FRAME)
    cos_part = np.cos(phases) / np.sqrt(FRAME)
    sin_part = -np.sin(phases) / np.sqrt(FRAME)
    table = np.concatenate([cos_part, sin_part], 1)
    return table.astype(jnp.bfloat16).astype(np.float32)


def stages_of(tiles):
    bits = tiles.bit_length() - 1
    assert tiles == 1 << bits
    stages, at, rows = [], 0, FRAME
    while at < bits:
        radix = 2 if at == 0 or bits - at == 1 else 4
        after = rows // radix if rows // radix >= MIN_ROWS else rows
        stages.append((at, radix, rows, after))
        rows = after
        at += 1 if radix == 2 else 2
    return stages


def tree(values, join):
    while len(values) > 1:
        values = [join(values[i], values[i + 1]) for i in range(0, len(values), 2)]
    return values[0]


def kernel(
    tiles,
    stages,
    obj,
    probe_given,
    frames_given,
    offsets,
    counts,
    table_given,
    obj_out,
    probe_out,
    probe,
    frames,
    table,
    fwd,
    inv,
    load_sem,
    ext,
    power_probe,
    ext_split,
    illum,
    illum_in,
    patches,
    far,
    power,
    power_in,
    factor,
    grad,
    grad_in,
    gext,
    spill_in,
    acc,
    peaks,
    halo_sem,
    relay_sem,
    pp_sem,
    illum_sem,
    power_sem,
    grad_sem,
    spill_sem,
    upd_sem,
    *staged,
):
    n_st = len(stages)
    rs_in, pk_in = staged[:n_st], staged[n_st : 2 * n_st]
    rs_sem, ag_sem, pk_sem = (staged[(2 + j) * n_st : (3 + j) * n_st] for j in range(3))
    slots = frames.shape[0]
    modes = probe.shape[0]
    f = FRAME
    me = lax.axis_index("tile")
    core = lax.axis_index("mode")
    other = 1 - core
    has_left, has_right = me > 0, me < tiles - 1
    left, right = jnp.maximum(me - 1, 0), jnp.minimum(me + 1, tiles - 1)

    def remote(src, dst, sems, **where):
        return pltpu.make_async_remote_copy(
            src_ref=src,
            dst_ref=dst,
            send_sem=sems[0],
            recv_sem=sems[1],
            device_id=where,
            device_id_type=pl.DeviceIdType.MESH,
        )

    def pair(sem, *at):
        return (sem.at[(0, *at)], sem.at[(1, *at)])

    loads = [
        pltpu.make_async_copy(src, dst, load_sem.at[j])
        for j, (src, dst) in enumerate(
            [
                (probe_given, probe),
                (obj, ext.at[:, pl.ds(0, f)]),
                (table_given, table),
                (frames_given, frames),
            ]
        )
    ]
    for load in loads:
        load.start()

    barrier = pltpu.get_barrier_semaphore()

    def greet(**where):
        pl.semaphore_signal(
            barrier, inc=1, device_id=where, device_id_type=pl.DeviceIdType.MESH
        )

    greet(mode=other)
    greeted = 1
    for at, radix, _, _ in stages:
        for d in range(1, radix):
            greet(tile=me ^ (d << at))
            greeted += 1

    @pl.when(has_left)
    def _():
        greet(tile=left)

    @pl.when(has_right)
    def _():
        greet(tile=right)

    beside = jnp.minimum(me, 1) + jnp.minimum(tiles - 1 - me, 1)
    pl.semaphore_wait(barrier, greeted + beside)

    halo = remote(obj.at[core], ext.at[core, pl.ds(f, f)], pair(halo_sem), tile=left)

    @pl.when(has_left)
    def _():
        halo.start()

    loads[0].wait()
    own_power = jnp.zeros((f, f), jnp.float32)
    for k in range(modes):
        own_power += probe[k, :, :f] ** 2 + probe[k, :, f:] ** 2
    power_probe[0] = own_power
    pp_copy = remote(power_probe.at[0], power_probe.at[1], pair(pp_sem), mode=other)
    pp_copy.start()

    def each(step):
        for s in range(slots):
            step(s, 0)

    def live(s):
        return jnp.clip(counts[0] - s, 0, 1).astype(jnp.float32)

    def dot(a, b):
        return jnp.dot(a, b, preferred_element_type=jnp.float32)

    def split(x):
        high = x.astype(jnp.bfloat16)
        return high, (x - high.astype(jnp.float32)).astype(jnp.bfloat16)

    def shifts(rows, columns, by):
        i = lax.broadcasted_iota(jnp.int32, (rows, columns), 0)
        j = lax.broadcasted_iota(jnp.int32, (rows, columns), 1)
        apart = j - i if rows < columns else i - j
        return jnp.where(apart == by, 1.0, 0.0).astype(jnp.float32)

    def spread(s, values):
        across = shifts(f, 2 * f, offsets[1, s]).astype(jnp.bfloat16)
        down = (shifts(2 * f, f, offsets[0, s]) * live(s)).astype(jnp.bfloat16)
        wide = dot(jnp.concatenate(split(values), 0), across).astype(jnp.bfloat16)
        return dot(jnp.concatenate([down, down], 1), wide)

    pp_copy.wait()
    probe_power = power_probe[0] + power_probe[1]
    illum[...] = jnp.zeros_like(illum)

    def light(s, carry):
        illum[...] += spread(s, probe_power)
        return carry

    each(light)
    illum_copy = remote(illum.at[pl.ds(f, f)], illum_in, pair(illum_sem), tile=right)

    @pl.when(has_right)
    def _():
        illum_copy.start()

    relay = remote(
        ext.at[core, pl.ds(f, f)], ext.at[core, pl.ds(f, f)], pair(relay_sem), mode=other
    )

    @pl.when(has_right)
    def _():
        halo.wait_recv()
        relay.start()
        relay.wait_recv()

    @pl.when(jnp.logical_not(has_right))
    def _():
        ext[:, f:, :] = jnp.zeros((2, f, 2 * f), jnp.float32)

    loads[1].wait()
    for part in range(2):
        for j, piece in enumerate(split(ext[part])):
            ext_split[:, (2 * part + j) * 2 * f : (2 * part + j + 1) * 2 * f] = piece

    def window(s):
        down = (shifts(f, 2 * f, offsets[0, s]) * live(s)).astype(jnp.bfloat16)
        across = shifts(2 * f, f, offsets[1, s]).astype(jnp.bfloat16)
        rows = dot(down, ext_split[...]).astype(jnp.bfloat16)
        both = jnp.concatenate([rows[:, : 4 * f], rows[:, 4 * f :]], 0)
        return dot(both, jnp.concatenate([across, across], 0))

    def swap(x):
        return jnp.concatenate(
            [
                jnp.concatenate([x[:f, :f], x[f:, :f]], 1),
                jnp.concatenate([x[:f, f:], x[f:, f:]], 1),
            ],
            0,
        )

    def power_copy(s):
        return remote(power.at[s], power_in.at[s], pair(power_sem, s), mode=other)

    def forward(s, carry):
        patch = window(s)
        xr, xi = patch[:f], patch[f:]
        patches[s, :, :f] = xr
        patches[s, :, f:] = xi
        total = jnp.zeros((f, f), jnp.float32)
        for p in range(modes // 2):
            psi = []
            for k in (2 * p, 2 * p + 1):
                pr, pi = probe[k, :, :f], probe[k, :, f:]
                psi.append(
                    jnp.concatenate([pr * xr - pi * xi, pr * xi + pi * xr], 1).astype(jnp.bfloat16)
                )
            half = dot(jnp.concatenate(psi, 0), fwd[...]).astype(jnp.bfloat16)
            wave = dot(inv[...], swap(half))
            far[s, p] = wave
            squares = wave * wave
            total += (squares[:f, :f] + squares[f:, :f]) + (squares[:f, f:] + squares[f:, f:])
        power[s] = total
        power_copy(s).start()
        return carry

    loads[2].wait()
    for ref, sign in ((fwd, 1.0), (inv, -1.0)):
        ref[:f, :f] = table[:, :f].astype(jnp.bfloat16)
        ref[f:, f:] = table[:, :f].astype(jnp.bfloat16)
        ref[:f, f:] = (sign * table[:, f:]).astype(jnp.bfloat16)
        ref[f:, :f] = (-sign * table[:, f:]).astype(jnp.bfloat16)
    each(forward)

    @pl.when(has_left)
    def _():
        illum_copy.wait_recv()

    @pl.when(jnp.logical_not(has_left))
    def _():
        illum_in[...] = jnp.zeros_like(illum_in)

    @pl.when(has_right)
    def _():
        illum_copy.wait_send()

    illum[:f] = illum[:f] + illum_in[...]
    high = jnp.max(illum[:f].reshape(f // 8, 8, 2 * f), 0)
    peaks[0] = jnp.maximum(high[:, :f], high[:, f:])

    def peak_copies(i):
        at, radix, _, _ = stages[i]
        return [
            remote(
                peaks.at[i], pk_in[i].at[d - 1], pair(pk_sem[i], d - 1), tile=me ^ (d << at)
            )
            for d in range(1, radix)
        ]

    def peak_start(i):
        for copy in peak_copies(i):
            copy.start()

    def peak_finish(i):
        for copy in peak_copies(i):
            copy.wait()
        radix = stages[i][1]
        peaks[i + 1] = tree([peaks[i]] + [pk_in[i][d] for d in range(radix - 1)], jnp.maximum)

    peak_start(0)

    def rescale(s, carry):
        power_copy(s).wait()
        factor[s] = (
            jnp.sqrt(frames[s]) * lax.rsqrt(power[s] + power_in[s] + 1.0) - 1.0
        )
        return carry

    loads[3].wait()
    each(rescale)

    starts = [0]
    for at, radix, rows, after in stages:
        digit = lax.rem(me // (1 << at), radix)
        starts.append(starts[-1] + digit * after if after < rows else starts[-1])

    def rows_at(ref, k, start, rows):
        return ref.at[k, pl.ds(pl.multiple_of(start, MIN_ROWS), rows)]

    def rs_copies(i, k):
        at, radix, rows, after = stages[i]
        digit = lax.rem(me // (1 << at), radix)
        copies = []
        for d in range(1, radix):
            start = starts[i] + (digit ^ d) * after if after < rows else starts[i]
            copies.append(
                remote(
                    rows_at(acc, k, start, after),
                    rs_in[i].at[k, d - 1],
                    pair(rs_sem[i], k, d - 1),
                    tile=me ^ (d << at),
                )
            )
        return copies

    def rs_start(i, ks):
        for k in ks:
            for copy in rs_copies(i, k):
                copy.start()

    def rs_finish(i, ks):
        after, radix = stages[i][3], stages[i][1]
        for k in ks:
            for copy in rs_copies(i, k):
                copy.wait()
            here = rows_at(acc, k, starts[i + 1], after)
            here[...] = tree(
                [here[...]] + [rs_in[i][k, d] for d in range(radix - 1)], lax.add
            )

    scale = 1.0 / np.sqrt(np.float32(tiles * slots))

    def finish_sum(ks):
        for k in ks:
            last = stages[-1][3]
            rows_at(probe_out, k, starts[-1], last)[...] = (
                rows_at(acc, k, starts[-1], last)[...] * scale
            )

    def ag_copies(i, k):
        at, radix, rows, after = stages[i]
        if after == rows:
            return []
        here = rows_at(probe_out, k, starts[i + 1], after)
        return [
            remote(here, here, pair(ag_sem[i], k, d - 1), tile=me ^ (d << at))
            for d in range(1, radix)
        ]

    def ag_start(i, ks):
        for k in ks:
            for copy in ag_copies(i, k):
                copy.start()

    def ag_finish(i, ks):
        for k in ks:
            for copy in ag_copies(i, k):
                copy.wait()

    groups = [(2 * p, 2 * p + 1) for p in range(modes // 2)]
    for p, ks in enumerate(groups):
        for k in ks:
            acc[k] = jnp.zeros((f, 2 * f), jnp.float32)

        def backward(s, carry, p=p, ks=ks):
            scaled = factor[s]
            wide = jnp.concatenate([scaled, scaled], 1)
            wide = jnp.concatenate([wide, wide], 0)
            corrected = (far[s, p] * wide).astype(jnp.bfloat16)
            half = dot(swap(corrected), inv[...]).astype(jnp.bfloat16)
            back = dot(fwd[...], swap(half))
            xr, xi = patches[s, :, :f], patches[s, :, f:]
            gr, gi = None, None
            for j, k in enumerate(ks):
                br, bi = back[:f, j * f : (j + 1) * f], back[f:, j * f : (j + 1) * f]
                pr, pi = probe[k, :, :f], probe[k, :, f:]
                r, i = pr * br + pi * bi, pr * bi - pi * br
                gr, gi = (r, i) if gr is None else (gr + r, gi + i)
                acc[k, :, :f] += xr * br + xi * bi
                acc[k, :, f:] += xr * bi - xi * br
            if p == 0:
                grad[0, s], grad[1, s] = gr, gi
            else:
                grad[0, s] += gr
                grad[1, s] += gi
            return carry

        each(backward)
        if p == len(groups) - 1:
            grad_copy = remote(grad.at[other], grad_in, pair(grad_sem), mode=other)
            grad_copy.start()
        rs_start(0, ks)
        if p < n_st:
            peak_finish(p)
            if p + 1 < n_st:
                peak_start(p + 1)

    for i in range(len(groups), n_st):
        peak_finish(i)
        if i + 1 < n_st:
            peak_start(i + 1)

    grad_copy.wait()
    gext[...] = jnp.zeros_like(gext)

    def gather_up(s, carry):
        gext[...] += spread(s, grad[core, s] + grad_in[s])
        return carry

    each(gather_up)
    spill_copy = remote(gext.at[pl.ds(f, f)], spill_in, pair(spill_sem), tile=right)

    @pl.when(has_right)
    def _():
        spill_copy.start()

    for i in range(n_st):
        for ks in groups:
            rs_finish(i, ks)
            if i + 1 < n_st:
                rs_start(i + 1, ks)
            else:
                finish_sum(ks)
                ag_start(i, ks)

    @pl.when(has_left)
    def _():
        spill_copy.wait_recv()

    @pl.when(jnp.logical_not(has_left))
    def _():
        spill_in[...] = jnp.zeros_like(spill_in)

    peak = jnp.max(peaks[n_st])
    obj_out[core] = ext[core, :f] + (gext[:f] + spill_in[...]) / (illum[:f] + 0.1 * peak)
    upd_copy = remote(obj_out.at[core], obj_out.at[core], pair(upd_sem), mode=other)
    upd_copy.start()

    for i in reversed(range(n_st)):
        for ks in groups:
            ag_finish(i, ks)
            if i > 0:
                ag_start(i - 1, ks)

    upd_copy.wait()

    @pl.when(has_left)
    def _():
        halo.wait_send()

    @pl.when(has_right)
    def _():
        relay.wait_send()
        spill_copy.wait_send()


def body(tiles, object_slab, probe_modes, frames, offsets, counts):
    f = FRAME
    stages = stages_of(tiles)
    slots, modes = frames.shape[0], probe_modes.shape[0]
    columns = object_slab.shape[2]
    table = dft_table()
    f32 = jnp.float32
    vmem = pl.BlockSpec(memory_space=pltpu.VMEM)
    hbm = pl.BlockSpec(memory_space=pltpu.HBM)
    smem = pl.BlockSpec(memory_space=pltpu.SMEM)
    dma = pltpu.SemaphoreType.DMA
    scratch = [
        pltpu.VMEM(probe_modes.shape, f32),
        pltpu.VMEM(frames.shape, f32),
        pltpu.VMEM(table.shape, f32),
        pltpu.VMEM((2 * f, 2 * f), jnp.bfloat16),
        pltpu.VMEM((2 * f, 2 * f), jnp.bfloat16),
        dma((4,)),
        pltpu.VMEM((2, 2 * f, columns), f32),
        pltpu.VMEM((2, f, f), f32),
        pltpu.VMEM((2 * f, 4 * columns), jnp.bfloat16),
        pltpu.VMEM((2 * f, columns), f32),
        pltpu.VMEM((f, columns), f32),
        pltpu.VMEM((slots, f, 2 * f), f32),
        pltpu.VMEM((slots, modes // 2, 2 * f, 2 * f), f32),
        pltpu.VMEM((slots, f, f), f32),
        pltpu.VMEM((slots, f, f), f32),
        pltpu.VMEM((slots, f, f), f32),
        pltpu.VMEM((2, slots, f, f), f32),
        pltpu.VMEM((slots, f, f), f32),
        pltpu.VMEM((2 * f, columns), f32),
        pltpu.VMEM((f, columns), f32),
        pltpu.VMEM((modes, f, 2 * f), f32),
        pltpu.VMEM((len(stages) + 1, 8, f), f32),
        dma((2,)),
        dma((2,)),
        dma((2,)),
        dma((2,)),
        dma((2, slots)),
        dma((2,)),
        dma((2,)),
        dma((2,)),
    ]
    scratch += [pltpu.VMEM((modes, radix - 1, after, 2 * f), f32) for _, radix, _, after in stages]
    scratch += [pltpu.VMEM((radix - 1, 8, f), f32) for _, radix, _, _ in stages]
    for _ in range(2):
        scratch += [dma((2, modes, radix - 1)) for _, radix, _, _ in stages]
    scratch += [dma((2, radix - 1)) for _, radix, _, _ in stages]
    updated, probe_direction = pl.pallas_call(
        functools.partial(kernel, tiles, stages),
        out_shape=(
            jax.ShapeDtypeStruct((2, f, columns), f32),
            jax.ShapeDtypeStruct((modes, f, 2 * f), f32),
        ),
        in_specs=[hbm, hbm, hbm, smem, smem, hbm],
        out_specs=(vmem, vmem),
        scratch_shapes=scratch,
        compiler_params=pltpu.CompilerParams(
            collective_id=0, has_side_effects=True, vmem_limit_bytes=60 * 1024 * 1024
        ),
        name="ptycho_step",
    )(object_slab.transpose(1, 0, 2), probe_modes, frames, offsets.T, counts, table)
    return updated.transpose(1, 0, 2), probe_direction


def solution(mesh):
    placed = (
        P(("grp", "tile"), None, None),
        P(("grp", "mode"), None, None),
        P(("grp", "tile"), None, None),
        P(("grp", "tile"), None),
        P(("grp", "tile")),
    )
    return jax.shard_map(
        functools.partial(body, mesh.shape["tile"]),
        mesh=mesh,
        in_specs=placed,
        out_specs=(P(("grp", "tile"), None, None), P(("grp", "mode"), None, None)),
        check_vma=False,
    )
```

```python
import functools

import jax
import jax.numpy as jnp
import numpy as np
from jax import lax
from jax.experimental import pallas as pl
from jax.experimental.pallas import tpu as pltpu
from jax.sharding import PartitionSpec as P

FRAME = 128
MIN_ROWS = 8


def dft_table():
    indices = np.arange(FRAME)
    phases = (indices[:, None] * indices[None, :] % FRAME) * (2.0 * np.pi / FRAME)
    cos_part = np.cos(phases) / np.sqrt(FRAME)
    sin_part = -np.sin(phases) / np.sqrt(FRAME)
    table = np.concatenate([cos_part, sin_part], 1)
    return table.astype(jnp.bfloat16).astype(np.float32)


def stages_of(tiles):
    bits = tiles.bit_length() - 1
    assert tiles == 1 << bits
    stages, at, rows = [], 0, FRAME
    while at < bits:
        radix = 2 if at == 0 or bits - at == 1 else 4
        after = rows // radix if rows // radix >= MIN_ROWS else rows
        stages.append((at, radix, rows, after))
        rows = after
        at += 1 if radix == 2 else 2
    return stages


def tree(values, join):
    while len(values) > 1:
        values = [join(values[i], values[i + 1]) for i in range(0, len(values), 2)]
    return values[0]


def kernel(
    tiles,
    stages,
    obj,
    probe_given,
    frames_given,
    offsets,
    counts,
    table_given,
    obj_out,
    probe_out,
    probe,
    frames,
    table,
    fwd,
    inv,
    load_sem,
    ext,
    power_probe,
    ext_split,
    illum,
    illum_in,
    patches,
    far,
    power,
    power_in,
    factor,
    grad,
    grad_in,
    gext,
    spill_in,
    acc,
    peaks,
    halo_sem,
    relay_sem,
    pp_sem,
    illum_sem,
    power_sem,
    grad_sem,
    spill_sem,
    upd_sem,
    *staged,
):
    n_st = len(stages)
    rs_in, pk_in = staged[:n_st], staged[n_st : 2 * n_st]
    rs_sem, ag_sem, pk_sem = (staged[(2 + j) * n_st : (3 + j) * n_st] for j in range(3))
    slots = frames.shape[0]
    modes = probe.shape[0]
    f = FRAME
    me = lax.axis_index("tile")
    core = lax.axis_index("mode")
    other = 1 - core
    has_left, has_right = me > 0, me < tiles - 1
    left, right = jnp.maximum(me - 1, 0), jnp.minimum(me + 1, tiles - 1)

    def remote(src, dst, sems, **where):
        return pltpu.make_async_remote_copy(
            src_ref=src,
            dst_ref=dst,
            send_sem=sems[0],
            recv_sem=sems[1],
            device_id=where,
            device_id_type=pl.DeviceIdType.MESH,
        )

    def pair(sem, *at):
        return (sem.at[(0, *at)], sem.at[(1, *at)])

    loads = [
        pltpu.make_async_copy(src, dst, load_sem.at[j])
        for j, (src, dst) in enumerate(
            [
                (probe_given, probe),
                (obj, ext.at[:, pl.ds(0, f)]),
                (table_given, table),
                (frames_given, frames),
            ]
        )
    ]
    for load in loads:
        load.start()

    barrier = pltpu.get_barrier_semaphore()

    def greet(**where):
        pl.semaphore_signal(
            barrier, inc=1, device_id=where, device_id_type=pl.DeviceIdType.MESH
        )

    greet(mode=other)
    greeted = 1
    for at, radix, _, _ in stages:
        for d in range(1, radix):
            greet(tile=me ^ (d << at))
            greeted += 1

    @pl.when(has_left)
    def _():
        greet(tile=left)

    @pl.when(has_right)
    def _():
        greet(tile=right)

    beside = jnp.minimum(me, 1) + jnp.minimum(tiles - 1 - me, 1)
    pl.semaphore_wait(barrier, greeted + beside)

    halo = remote(obj.at[core], ext.at[core, pl.ds(f, f)], pair(halo_sem), tile=left)

    @pl.when(has_left)
    def _():
        halo.start()

    loads[0].wait()
    own_power = jnp.zeros((f, f), jnp.float32)
    for k in range(modes):
        own_power += probe[k, :, :f] ** 2 + probe[k, :, f:] ** 2
    power_probe[0] = own_power
    pp_copy = remote(power_probe.at[0], power_probe.at[1], pair(pp_sem), mode=other)
    pp_copy.start()

    def each(step):
        for s in range(slots):
            step(s, 0)

    def live(s):
        return jnp.clip(counts[0] - s, 0, 1).astype(jnp.float32)

    def dot(a, b):
        return jnp.dot(a, b, preferred_element_type=jnp.float32)

    def split(x):
        high = x.astype(jnp.bfloat16)
        return high, (x - high.astype(jnp.float32)).astype(jnp.bfloat16)

    def shifts(rows, columns, by):
        i = lax.broadcasted_iota(jnp.int32, (rows, columns), 0)
        j = lax.broadcasted_iota(jnp.int32, (rows, columns), 1)
        apart = j - i if rows < columns else i - j
        return jnp.where(apart == by, 1.0, 0.0).astype(jnp.float32)

    def spread(s, values):
        across = shifts(f, 2 * f, offsets[1, s]).astype(jnp.bfloat16)
        down = (shifts(2 * f, f, offsets[0, s]) * live(s)).astype(jnp.bfloat16)
        wide = dot(jnp.concatenate(split(values), 0), across).astype(jnp.bfloat16)
        return dot(jnp.concatenate([down, down], 1), wide)

    pp_copy.wait()
    probe_power = power_probe[0] + power_probe[1]
    illum[...] = jnp.zeros_like(illum)

    def light(s, carry):
        illum[...] += spread(s, probe_power)
        return carry

    each(light)
    illum_copy = remote(illum.at[pl.ds(f, f)], illum_in, pair(illum_sem), tile=right)

    @pl.when(has_right)
    def _():
        illum_copy.start()

    relay = remote(
        ext.at[core, pl.ds(f, f)], ext.at[core, pl.ds(f, f)], pair(relay_sem), mode=other
    )

    @pl.when(has_right)
    def _():
        halo.wait_recv()
        relay.start()
        relay.wait_recv()

    @pl.when(jnp.logical_not(has_right))
    def _():
        ext[:, f:, :] = jnp.zeros((2, f, 2 * f), jnp.float32)

    loads[1].wait()
    for part in range(2):
        for j, piece in enumerate(split(ext[part])):
            ext_split[:, (2 * part + j) * 2 * f : (2 * part + j + 1) * 2 * f] = piece

    def window(s):
        down = (shifts(f, 2 * f, offsets[0, s]) * live(s)).astype(jnp.bfloat16)
        across = shifts(2 * f, f, offsets[1, s]).astype(jnp.bfloat16)
        rows = dot(down, ext_split[...]).astype(jnp.bfloat16)
        both = jnp.concatenate([rows[:, : 4 * f], rows[:, 4 * f :]], 0)
        return dot(both, jnp.concatenate([across, across], 0))

    def swap(x):
        return jnp.concatenate(
            [
                jnp.concatenate([x[:f, :f], x[f:, :f]], 1),
                jnp.concatenate([x[:f, f:], x[f:, f:]], 1),
            ],
            0,
        )

    def power_copy(s):
        return remote(power.at[s], power_in.at[s], pair(power_sem, s), mode=other)

    def forward(s, carry):
        patch = window(s)
        xr, xi = patch[:f], patch[f:]
        patches[s, :, :f] = xr
        patches[s, :, f:] = xi
        total = jnp.zeros((f, f), jnp.float32)
        for p in range(modes // 2):
            psi = []
            for k in (2 * p, 2 * p + 1):
                pr, pi = probe[k, :, :f], probe[k, :, f:]
                psi.append(
                    jnp.concatenate([pr * xr - pi * xi, pr * xi + pi * xr], 1).astype(jnp.bfloat16)
                )
            half = dot(jnp.concatenate(psi, 0), fwd[...]).astype(jnp.bfloat16)
            wave = dot(inv[...], swap(half))
            far[s, p] = wave
            squares = wave * wave
            total += (squares[:f, :f] + squares[f:, :f]) + (squares[:f, f:] + squares[f:, f:])
        power[s] = total
        power_copy(s).start()
        return carry

    loads[2].wait()
    for ref, sign in ((fwd, 1.0), (inv, -1.0)):
        ref[:f, :f] = table[:, :f].astype(jnp.bfloat16)
        ref[f:, f:] = table[:, :f].astype(jnp.bfloat16)
        ref[:f, f:] = (sign * table[:, f:]).astype(jnp.bfloat16)
        ref[f:, :f] = (-sign * table[:, f:]).astype(jnp.bfloat16)
    each(forward)

    @pl.when(has_left)
    def _():
        illum_copy.wait_recv()

    @pl.when(jnp.logical_not(has_left))
    def _():
        illum_in[...] = jnp.zeros_like(illum_in)

    @pl.when(has_right)
    def _():
        illum_copy.wait_send()

    illum[:f] = illum[:f] + illum_in[...]
    high = jnp.max(illum[:f].reshape(f // 8, 8, 2 * f), 0)
    peaks[0] = jnp.maximum(high[:, :f], high[:, f:])

    def peak_copies(i):
        at, radix, _, _ = stages[i]
        return [
            remote(
                peaks.at[i], pk_in[i].at[d - 1], pair(pk_sem[i], d - 1), tile=me ^ (d << at)
            )
            for d in range(1, radix)
        ]

    def peak_start(i):
        for copy in peak_copies(i):
            copy.start()

    def peak_finish(i):
        for copy in peak_copies(i):
            copy.wait()
        radix = stages[i][1]
        peaks[i + 1] = tree([peaks[i]] + [pk_in[i][d] for d in range(radix - 1)], jnp.maximum)

    peak_start(0)

    def rescale(s, carry):
        power_copy(s).wait()
        factor[s] = (
            jnp.sqrt(frames[s]) * lax.rsqrt(power[s] + power_in[s] + 1.0) - 1.0
        )
        return carry

    loads[3].wait()
    each(rescale)

    starts = [0]
    for at, radix, rows, after in stages:
        digit = lax.rem(me // (1 << at), radix)
        starts.append(starts[-1] + digit * after if after < rows else starts[-1])

    def rows_at(ref, k, start, rows):
        return ref.at[k, pl.ds(pl.multiple_of(start, MIN_ROWS), rows)]

    def rs_copies(i, k):
        at, radix, rows, after = stages[i]
        digit = lax.rem(me // (1 << at), radix)
        copies = []
        for d in range(1, radix):
            start = starts[i] + (digit ^ d) * after if after < rows else starts[i]
            copies.append(
                remote(
                    rows_at(acc, k, start, after),
                    rs_in[i].at[k, d - 1],
                    pair(rs_sem[i], k, d - 1),
                    tile=me ^ (d << at),
                )
            )
        return copies

    def rs_start(i, ks):
        for k in ks:
            for copy in rs_copies(i, k):
                copy.start()

    def rs_finish(i, ks):
        after, radix = stages[i][3], stages[i][1]
        for k in ks:
            for copy in rs_copies(i, k):
                copy.wait()
            here = rows_at(acc, k, starts[i + 1], after)
            here[...] = tree(
                [here[...]] + [rs_in[i][k, d] for d in range(radix - 1)], lax.add
            )

    scale = 1.0 / np.sqrt(np.float32(tiles * slots))

    def finish_sum(ks):
        for k in ks:
            last = stages[-1][3]
            rows_at(probe_out, k, starts[-1], last)[...] = (
                rows_at(acc, k, starts[-1], last)[...] * scale
            )

    def ag_copies(i, k):
        at, radix, rows, after = stages[i]
        if after == rows:
            return []
        here = rows_at(probe_out, k, starts[i + 1], after)
        return [
            remote(here, here, pair(ag_sem[i], k, d - 1), tile=me ^ (d << at))
            for d in range(1, radix)
        ]

    def ag_start(i, ks):
        for k in ks:
            for copy in ag_copies(i, k):
                copy.start()

    def ag_finish(i, ks):
        for k in ks:
            for copy in ag_copies(i, k):
                copy.wait()

    groups = [(2 * p, 2 * p + 1) for p in range(modes // 2)]
    for p, ks in enumerate(groups):
        for k in ks:
            acc[k] = jnp.zeros((f, 2 * f), jnp.float32)

        def backward(s, carry, p=p, ks=ks):
            scaled = factor[s]
            wide = jnp.concatenate([scaled, scaled], 1)
            wide = jnp.concatenate([wide, wide], 0)
            corrected = (far[s, p] * wide).astype(jnp.bfloat16)
            half = dot(swap(corrected), inv[...]).astype(jnp.bfloat16)
            back = dot(fwd[...], swap(half))
            xr, xi = patches[s, :, :f], patches[s, :, f:]
            gr, gi = None, None
            for j, k in enumerate(ks):
                br, bi = back[:f, j * f : (j + 1) * f], back[f:, j * f : (j + 1) * f]
                pr, pi = probe[k, :, :f], probe[k, :, f:]
                r, i = pr * br + pi * bi, pr * bi - pi * br
                gr, gi = (r, i) if gr is None else (gr + r, gi + i)
                acc[k, :, :f] += xr * br + xi * bi
                acc[k, :, f:] += xr * bi - xi * br
            if p == 0:
                grad[0, s], grad[1, s] = gr, gi
            else:
                grad[0, s] += gr
                grad[1, s] += gi
            return carry

        each(backward)
        if p == len(groups) - 1:
            grad_copy = remote(grad.at[other], grad_in, pair(grad_sem), mode=other)
            grad_copy.start()
        rs_start(0, ks)
        if p < n_st:
            peak_finish(p)
            if p + 1 < n_st:
                peak_start(p + 1)

    for i in range(len(groups), n_st):
        peak_finish(i)
        if i + 1 < n_st:
            peak_start(i + 1)

    def advance(i, k):
        rs_finish(i, (k,))
        if i + 1 < n_st:
            rs_start(i + 1, (k,))
        else:
            finish_sum((k,))
            ag_start(i, (k,))

    early = groups[0]
    for k in early:
        advance(0, k)

    grad_copy.wait()
    gext[...] = jnp.zeros_like(gext)

    def gather_up(s, carry):
        gext[...] += spread(s, grad[core, s] + grad_in[s])
        return carry

    each(gather_up)
    spill_copy = remote(gext.at[pl.ds(f, f)], spill_in, pair(spill_sem), tile=right)

    @pl.when(has_right)
    def _():
        spill_copy.start()

    for i in range(n_st):
        for k in range(modes):
            if i > 0 or k not in early:
                advance(i, k)

    @pl.when(has_left)
    def _():
        spill_copy.wait_recv()

    @pl.when(jnp.logical_not(has_left))
    def _():
        spill_in[...] = jnp.zeros_like(spill_in)

    peak = jnp.max(peaks[n_st])
    obj_out[core] = ext[core, :f] + (gext[:f] + spill_in[...]) / (illum[:f] + 0.1 * peak)
    upd_copy = remote(obj_out.at[core], obj_out.at[core], pair(upd_sem), mode=other)
    upd_copy.start()

    for i in reversed(range(n_st)):
        for k in range(modes):
            ag_finish(i, (k,))
            if i > 0:
                ag_start(i - 1, (k,))

    upd_copy.wait()

    @pl.when(has_left)
    def _():
        halo.wait_send()

    @pl.when(has_right)
    def _():
        relay.wait_send()
        spill_copy.wait_send()


def body(tiles, object_slab, probe_modes, frames, offsets, counts):
    f = FRAME
    stages = stages_of(tiles)
    slots, modes = frames.shape[0], probe_modes.shape[0]
    columns = object_slab.shape[2]
    table = dft_table()
    f32 = jnp.float32
    vmem = pl.BlockSpec(memory_space=pltpu.VMEM)
    hbm = pl.BlockSpec(memory_space=pltpu.HBM)
    smem = pl.BlockSpec(memory_space=pltpu.SMEM)
    dma = pltpu.SemaphoreType.DMA
    scratch = [
        pltpu.VMEM(probe_modes.shape, f32),
        pltpu.VMEM(frames.shape, f32),
        pltpu.VMEM(table.shape, f32),
        pltpu.VMEM((2 * f, 2 * f), jnp.bfloat16),
        pltpu.VMEM((2 * f, 2 * f), jnp.bfloat16),
        dma((4,)),
        pltpu.VMEM((2, 2 * f, columns), f32),
        pltpu.VMEM((2, f, f), f32),
        pltpu.VMEM((2 * f, 4 * columns), jnp.bfloat16),
        pltpu.VMEM((2 * f, columns), f32),
        pltpu.VMEM((f, columns), f32),
        pltpu.VMEM((slots, f, 2 * f), f32),
        pltpu.VMEM((slots, modes // 2, 2 * f, 2 * f), f32),
        pltpu.VMEM((slots, f, f), f32),
        pltpu.VMEM((slots, f, f), f32),
        pltpu.VMEM((slots, f, f), f32),
        pltpu.VMEM((2, slots, f, f), f32),
        pltpu.VMEM((slots, f, f), f32),
        pltpu.VMEM((2 * f, columns), f32),
        pltpu.VMEM((f, columns), f32),
        pltpu.VMEM((modes, f, 2 * f), f32),
        pltpu.VMEM((len(stages) + 1, 8, f), f32),
        dma((2,)),
        dma((2,)),
        dma((2,)),
        dma((2,)),
        dma((2, slots)),
        dma((2,)),
        dma((2,)),
        dma((2,)),
    ]
    scratch += [pltpu.VMEM((modes, radix - 1, after, 2 * f), f32) for _, radix, _, after in stages]
    scratch += [pltpu.VMEM((radix - 1, 8, f), f32) for _, radix, _, _ in stages]
    for _ in range(2):
        scratch += [dma((2, modes, radix - 1)) for _, radix, _, _ in stages]
    scratch += [dma((2, radix - 1)) for _, radix, _, _ in stages]
    updated, probe_direction = pl.pallas_call(
        functools.partial(kernel, tiles, stages),
        out_shape=(
            jax.ShapeDtypeStruct((2, f, columns), f32),
            jax.ShapeDtypeStruct((modes, f, 2 * f), f32),
        ),
        in_specs=[hbm, hbm, hbm, smem, smem, hbm],
        out_specs=(vmem, vmem),
        scratch_shapes=scratch,
        compiler_params=pltpu.CompilerParams(
            collective_id=0, has_side_effects=True, vmem_limit_bytes=60 * 1024 * 1024
        ),
        name="ptycho_step",
    )(object_slab.transpose(1, 0, 2), probe_modes, frames, offsets.T, counts, table)
    return updated.transpose(1, 0, 2), probe_direction


def solution(mesh):
    placed = (
        P(("grp", "tile"), None, None),
        P(("grp", "mode"), None, None),
        P(("grp", "tile"), None, None),
        P(("grp", "tile"), None),
        P(("grp", "tile")),
    )
    return jax.shard_map(
        functools.partial(body, mesh.shape["tile"]),
        mesh=mesh,
        in_specs=placed,
        out_specs=(P(("grp", "tile"), None, None), P(("grp", "mode"), None, None)),
        check_vma=False,
    )
```

```python
import functools

import jax
import jax.numpy as jnp
import numpy as np
from jax import lax
from jax.experimental import pallas as pl
from jax.experimental.pallas import tpu as pltpu
from jax.sharding import PartitionSpec as P

FRAME = 128
MIN_ROWS = 8


def dft_table():
    indices = np.arange(FRAME)
    phases = (indices[:, None] * indices[None, :] % FRAME) * (2.0 * np.pi / FRAME)
    cos_part = np.cos(phases) / np.sqrt(FRAME)
    sin_part = -np.sin(phases) / np.sqrt(FRAME)
    table = np.concatenate([cos_part, sin_part], 1)
    return table.astype(jnp.bfloat16).astype(np.float32)


def stages_of(tiles):
    bits = tiles.bit_length() - 1
    assert tiles == 1 << bits
    stages, at, rows = [], 0, FRAME
    while at < bits:
        radix = 2 if at == 0 or bits - at == 1 else 4
        after = rows // radix if rows // radix >= MIN_ROWS else rows
        stages.append((at, radix, rows, after))
        rows = after
        at += 1 if radix == 2 else 2
    return stages


def tree(values, join):
    while len(values) > 1:
        values = [join(values[i], values[i + 1]) for i in range(0, len(values), 2)]
    return values[0]


def kernel(
    tiles,
    stages,
    obj,
    probe_given,
    frames_given,
    offsets,
    counts,
    table_given,
    obj_out,
    probe_out,
    probe,
    frames,
    table,
    fwd,
    inv,
    load_sem,
    ext,
    updated,
    power_probe,
    ext_split,
    illum,
    illum_in,
    patches,
    far,
    power,
    power_in,
    factor,
    grad,
    grad_in,
    gext,
    spill_in,
    acc,
    peaks,
    halo_sem,
    relay_sem,
    pp_sem,
    illum_sem,
    power_sem,
    grad_sem,
    spill_sem,
    upd_sem,
    *staged,
):
    n_st = len(stages)
    rs_in, pk_in = staged[:n_st], staged[n_st : 2 * n_st]
    rs_sem, ag_sem, pk_sem = (staged[(2 + j) * n_st : (3 + j) * n_st] for j in range(3))
    slots = frames.shape[0]
    modes = probe.shape[0]
    f = FRAME
    me = lax.axis_index("tile")
    core = lax.axis_index("mode")
    other = 1 - core
    has_left, has_right = me > 0, me < tiles - 1
    left, right = jnp.maximum(me - 1, 0), jnp.minimum(me + 1, tiles - 1)

    def remote(src, dst, sems, **where):
        return pltpu.make_async_remote_copy(
            src_ref=src,
            dst_ref=dst,
            send_sem=sems[0],
            recv_sem=sems[1],
            device_id=where,
            device_id_type=pl.DeviceIdType.MESH,
        )

    def pair(sem, *at):
        return (sem.at[(0, *at)], sem.at[(1, *at)])

    loads = [
        pltpu.make_async_copy(src, dst, load_sem.at[j])
        for j, (src, dst) in enumerate(
            [
                (probe_given, probe),
                (obj, ext.at[pl.ds(0, f)]),
                (table_given, table),
                (frames_given, frames),
            ]
        )
    ]
    for load in loads:
        load.start()

    barrier = pltpu.get_barrier_semaphore()

    def greet(**where):
        pl.semaphore_signal(
            barrier, inc=1, device_id=where, device_id_type=pl.DeviceIdType.MESH
        )

    greet(mode=other)
    greeted = 1
    for at, radix, _, _ in stages:
        for d in range(1, radix):
            greet(tile=me ^ (d << at))
            greeted += 1

    @pl.when(has_left)
    def _():
        greet(tile=left)

    @pl.when(has_right)
    def _():
        greet(tile=right)

    beside = jnp.minimum(me, 1) + jnp.minimum(tiles - 1 - me, 1)
    pl.semaphore_wait(barrier, greeted + beside)

    half_rows = f // 2
    landed = ext.at[pl.ds(f + core * half_rows, half_rows)]
    halo = remote(
        obj.at[pl.ds(core * half_rows, half_rows)], landed, pair(halo_sem), tile=left
    )

    @pl.when(has_left)
    def _():
        halo.start()

    loads[0].wait()
    own_power = jnp.zeros((f, f), jnp.float32)
    for k in range(modes):
        own_power += probe[k, :, :f] ** 2 + probe[k, :, f:] ** 2
    power_probe[0] = own_power
    pp_copy = remote(power_probe.at[0], power_probe.at[1], pair(pp_sem), mode=other)
    pp_copy.start()

    def each(step):
        for s in range(slots):
            step(s, 0)

    def live(s):
        return jnp.clip(counts[0] - s, 0, 1).astype(jnp.float32)

    def dot(a, b):
        return jnp.dot(a, b, preferred_element_type=jnp.float32)

    def split(x):
        high = x.astype(jnp.bfloat16)
        return high, (x - high.astype(jnp.float32)).astype(jnp.bfloat16)

    def shifts(rows, columns, by):
        i = lax.broadcasted_iota(jnp.int32, (rows, columns), 0)
        j = lax.broadcasted_iota(jnp.int32, (rows, columns), 1)
        apart = j - i if rows < columns else i - j
        return jnp.where(apart == by, 1.0, 0.0).astype(jnp.float32)

    def spread(s, values):
        across = shifts(f, 2 * f, offsets[1, s]).astype(jnp.bfloat16)
        down = (shifts(2 * f, f, offsets[0, s]) * live(s)).astype(jnp.bfloat16)
        wide = dot(jnp.concatenate(split(values), 0), across).astype(jnp.bfloat16)
        return dot(jnp.concatenate([down, down], 1), wide)

    pp_copy.wait()
    probe_power = power_probe[0] + power_probe[1]
    illum[...] = jnp.zeros_like(illum)

    def light(s, carry):
        illum[...] += spread(s, probe_power)
        return carry

    each(light)
    illum_copy = remote(illum.at[pl.ds(f, f)], illum_in, pair(illum_sem), tile=right)

    @pl.when(has_right)
    def _():
        illum_copy.start()

    relay = remote(landed, landed, pair(relay_sem), mode=other)

    @pl.when(has_right)
    def _():
        halo.wait_recv()
        relay.start()
        relay.wait_recv()

    @pl.when(jnp.logical_not(has_right))
    def _():
        ext[f:] = jnp.zeros((f, 2, 2 * f), jnp.float32)

    loads[1].wait()
    for part in range(2):
        for j, piece in enumerate(split(ext[:, part, :])):
            ext_split[:, (2 * part + j) * 2 * f : (2 * part + j + 1) * 2 * f] = piece

    def window(s):
        down = (shifts(f, 2 * f, offsets[0, s]) * live(s)).astype(jnp.bfloat16)
        across = shifts(2 * f, f, offsets[1, s]).astype(jnp.bfloat16)
        rows = dot(down, ext_split[...]).astype(jnp.bfloat16)
        both = jnp.concatenate([rows[:, : 4 * f], rows[:, 4 * f :]], 0)
        return dot(both, jnp.concatenate([across, across], 0))

    def swap(x):
        return jnp.concatenate(
            [
                jnp.concatenate([x[:f, :f], x[f:, :f]], 1),
                jnp.concatenate([x[:f, f:], x[f:, f:]], 1),
            ],
            0,
        )

    def power_copy(s):
        return remote(power.at[s], power_in.at[s], pair(power_sem, s), mode=other)

    def forward(s, carry):
        patch = window(s)
        xr, xi = patch[:f], patch[f:]
        patches[s, :, :f] = xr
        patches[s, :, f:] = xi
        total = jnp.zeros((f, f), jnp.float32)
        for p in range(modes // 2):
            psi = []
            for k in (2 * p, 2 * p + 1):
                pr, pi = probe[k, :, :f], probe[k, :, f:]
                psi.append(
                    jnp.concatenate([pr * xr - pi * xi, pr * xi + pi * xr], 1).astype(jnp.bfloat16)
                )
            half = dot(jnp.concatenate(psi, 0), fwd[...]).astype(jnp.bfloat16)
            wave = dot(inv[...], swap(half))
            far[s, p] = wave
            squares = wave * wave
            total += (squares[:f, :f] + squares[f:, :f]) + (squares[:f, f:] + squares[f:, f:])
        power[s] = total
        power_copy(s).start()
        return carry

    loads[2].wait()
    for ref, sign in ((fwd, 1.0), (inv, -1.0)):
        ref[:f, :f] = table[:, :f].astype(jnp.bfloat16)
        ref[f:, f:] = table[:, :f].astype(jnp.bfloat16)
        ref[:f, f:] = (sign * table[:, f:]).astype(jnp.bfloat16)
        ref[f:, :f] = (-sign * table[:, f:]).astype(jnp.bfloat16)
    each(forward)

    @pl.when(has_left)
    def _():
        illum_copy.wait_recv()

    @pl.when(jnp.logical_not(has_left))
    def _():
        illum_in[...] = jnp.zeros_like(illum_in)

    @pl.when(has_right)
    def _():
        illum_copy.wait_send()

    illum[:f] = illum[:f] + illum_in[...]
    high = jnp.max(illum[:f].reshape(f // 8, 8, 2 * f), 0)
    peaks[0] = jnp.maximum(high[:, :f], high[:, f:])

    def peak_copies(i):
        at, radix, _, _ = stages[i]
        return [
            remote(
                peaks.at[i], pk_in[i].at[d - 1], pair(pk_sem[i], d - 1), tile=me ^ (d << at)
            )
            for d in range(1, radix)
        ]

    def peak_start(i):
        for copy in peak_copies(i):
            copy.start()

    def peak_finish(i):
        for copy in peak_copies(i):
            copy.wait()
        radix = stages[i][1]
        peaks[i + 1] = tree([peaks[i]] + [pk_in[i][d] for d in range(radix - 1)], jnp.maximum)

    peak_start(0)

    def rescale(s, carry):
        power_copy(s).wait()
        factor[s] = (
            jnp.sqrt(frames[s]) * lax.rsqrt(power[s] + power_in[s] + 1.0) - 1.0
        )
        return carry

    loads[3].wait()
    each(rescale)

    starts = [0]
    for at, radix, rows, after in stages:
        digit = lax.rem(me // (1 << at), radix)
        starts.append(starts[-1] + digit * after if after < rows else starts[-1])

    def rows_at(ref, k, start, rows):
        return ref.at[k, pl.ds(pl.multiple_of(start, MIN_ROWS), rows)]

    def rs_copies(i, k):
        at, radix, rows, after = stages[i]
        digit = lax.rem(me // (1 << at), radix)
        copies = []
        for d in range(1, radix):
            start = starts[i] + (digit ^ d) * after if after < rows else starts[i]
            copies.append(
                remote(
                    rows_at(acc, k, start, after),
                    rs_in[i].at[k, d - 1],
                    pair(rs_sem[i], k, d - 1),
                    tile=me ^ (d << at),
                )
            )
        return copies

    def rs_start(i, ks):
        for k in ks:
            for copy in rs_copies(i, k):
                copy.start()

    def rs_finish(i, ks):
        after, radix = stages[i][3], stages[i][1]
        for k in ks:
            for copy in rs_copies(i, k):
                copy.wait()
            here = rows_at(acc, k, starts[i + 1], after)
            here[...] = tree(
                [here[...]] + [rs_in[i][k, d] for d in range(radix - 1)], lax.add
            )

    scale = 1.0 / np.sqrt(np.float32(tiles * slots))

    def finish_sum(ks):
        for k in ks:
            last = stages[-1][3]
            rows_at(probe_out, k, starts[-1], last)[...] = (
                rows_at(acc, k, starts[-1], last)[...] * scale
            )

    def ag_copies(i, k):
        at, radix, rows, after = stages[i]
        if after == rows:
            return []
        here = rows_at(probe_out, k, starts[i + 1], after)
        return [
            remote(here, here, pair(ag_sem[i], k, d - 1), tile=me ^ (d << at))
            for d in range(1, radix)
        ]

    def ag_start(i, ks):
        for k in ks:
            for copy in ag_copies(i, k):
                copy.start()

    def ag_finish(i, ks):
        for k in ks:
            for copy in ag_copies(i, k):
                copy.wait()

    groups = [(2 * p, 2 * p + 1) for p in range(modes // 2)]
    for p, ks in enumerate(groups):
        for k in ks:
            acc[k] = jnp.zeros((f, 2 * f), jnp.float32)

        def backward(s, carry, p=p, ks=ks):
            scaled = factor[s]
            wide = jnp.concatenate([scaled, scaled], 1)
            wide = jnp.concatenate([wide, wide], 0)
            corrected = (far[s, p] * wide).astype(jnp.bfloat16)
            half = dot(swap(corrected), inv[...]).astype(jnp.bfloat16)
            back = dot(fwd[...], swap(half))
            xr, xi = patches[s, :, :f], patches[s, :, f:]
            gr, gi = None, None
            for j, k in enumerate(ks):
                br, bi = back[:f, j * f : (j + 1) * f], back[f:, j * f : (j + 1) * f]
                pr, pi = probe[k, :, :f], probe[k, :, f:]
                r, i = pr * br + pi * bi, pr * bi - pi * br
                gr, gi = (r, i) if gr is None else (gr + r, gi + i)
                acc[k, :, :f] += xr * br + xi * bi
                acc[k, :, f:] += xr * bi - xi * br
            if p == 0:
                grad[0, s], grad[1, s] = gr, gi
            else:
                grad[0, s] += gr
                grad[1, s] += gi
            return carry

        each(backward)
        if p == len(groups) - 1:
            grad_copy = remote(grad.at[other], grad_in, pair(grad_sem), mode=other)
            grad_copy.start()
        rs_start(0, ks)
        if p < n_st:
            peak_finish(p)
            if p + 1 < n_st:
                peak_start(p + 1)

    for i in range(len(groups), n_st):
        peak_finish(i)
        if i + 1 < n_st:
            peak_start(i + 1)

    def advance(i, k):
        rs_finish(i, (k,))
        if i + 1 < n_st:
            rs_start(i + 1, (k,))
        else:
            finish_sum((k,))
            ag_start(i, (k,))

    early = groups[0]
    for k in early:
        advance(0, k)

    grad_copy.wait()
    gext[...] = jnp.zeros_like(gext)

    def gather_up(s, carry):
        gext[...] += spread(s, grad[core, s] + grad_in[s])
        return carry

    each(gather_up)
    spill_copy = remote(gext.at[pl.ds(f, f)], spill_in, pair(spill_sem), tile=right)

    @pl.when(has_right)
    def _():
        spill_copy.start()

    for i in range(n_st):
        for k in range(modes):
            if i > 0 or k not in early:
                advance(i, k)

    @pl.when(has_left)
    def _():
        spill_copy.wait_recv()

    @pl.when(jnp.logical_not(has_left))
    def _():
        spill_in[...] = jnp.zeros_like(spill_in)

    peak = jnp.max(peaks[n_st])
    here = jnp.where(core == 0, ext[:f, 0, :], ext[:f, 1, :])
    updated[core] = here + (gext[:f] + spill_in[...]) / (illum[:f] + 0.1 * peak)
    upd_copy = remote(updated.at[core], updated.at[core], pair(upd_sem), mode=other)
    upd_copy.start()

    for i in reversed(range(n_st)):
        if i == 0:
            upd_copy.wait()
            for part in range(2):
                obj_out[:, part, :] = updated[part]
        for k in range(modes):
            ag_finish(i, (k,))
            if i > 0:
                ag_start(i - 1, (k,))

    @pl.when(has_left)
    def _():
        halo.wait_send()

    @pl.when(has_right)
    def _():
        relay.wait_send()
        spill_copy.wait_send()


def body(tiles, object_slab, probe_modes, frames, offsets, counts):
    f = FRAME
    stages = stages_of(tiles)
    slots, modes = frames.shape[0], probe_modes.shape[0]
    columns = object_slab.shape[2]
    table = dft_table()
    f32 = jnp.float32
    vmem = pl.BlockSpec(memory_space=pltpu.VMEM)
    hbm = pl.BlockSpec(memory_space=pltpu.HBM)
    smem = pl.BlockSpec(memory_space=pltpu.SMEM)
    dma = pltpu.SemaphoreType.DMA
    scratch = [
        pltpu.VMEM(probe_modes.shape, f32),
        pltpu.VMEM(frames.shape, f32),
        pltpu.VMEM(table.shape, f32),
        pltpu.VMEM((2 * f, 2 * f), jnp.bfloat16),
        pltpu.VMEM((2 * f, 2 * f), jnp.bfloat16),
        dma((4,)),
        pltpu.VMEM((2 * f, 2, columns), f32),
        pltpu.VMEM((2, f, columns), f32),
        pltpu.VMEM((2, f, f), f32),
        pltpu.VMEM((2 * f, 4 * columns), jnp.bfloat16),
        pltpu.VMEM((2 * f, columns), f32),
        pltpu.VMEM((f, columns), f32),
        pltpu.VMEM((slots, f, 2 * f), f32),
        pltpu.VMEM((slots, modes // 2, 2 * f, 2 * f), f32),
        pltpu.VMEM((slots, f, f), f32),
        pltpu.VMEM((slots, f, f), f32),
        pltpu.VMEM((slots, f, f), f32),
        pltpu.VMEM((2, slots, f, f), f32),
        pltpu.VMEM((slots, f, f), f32),
        pltpu.VMEM((2 * f, columns), f32),
        pltpu.VMEM((f, columns), f32),
        pltpu.VMEM((modes, f, 2 * f), f32),
        pltpu.VMEM((len(stages) + 1, 8, f), f32),
        dma((2,)),
        dma((2,)),
        dma((2,)),
        dma((2,)),
        dma((2, slots)),
        dma((2,)),
        dma((2,)),
        dma((2,)),
    ]
    scratch += [pltpu.VMEM((modes, radix - 1, after, 2 * f), f32) for _, radix, _, after in stages]
    scratch += [pltpu.VMEM((radix - 1, 8, f), f32) for _, radix, _, _ in stages]
    for _ in range(2):
        scratch += [dma((2, modes, radix - 1)) for _, radix, _, _ in stages]
    scratch += [dma((2, radix - 1)) for _, radix, _, _ in stages]
    return pl.pallas_call(
        functools.partial(kernel, tiles, stages),
        out_shape=(
            jax.ShapeDtypeStruct((f, 2, columns), f32),
            jax.ShapeDtypeStruct((modes, f, 2 * f), f32),
        ),
        in_specs=[hbm, hbm, hbm, smem, smem, hbm],
        out_specs=(vmem, vmem),
        scratch_shapes=scratch,
        compiler_params=pltpu.CompilerParams(
            collective_id=0, has_side_effects=True, vmem_limit_bytes=60 * 1024 * 1024
        ),
        name="ptycho_step",
    )(object_slab, probe_modes, frames, offsets.T, counts, table)


def solution(mesh):
    placed = (
        P(("grp", "tile"), None, None),
        P(("grp", "mode"), None, None),
        P(("grp", "tile"), None, None),
        P(("grp", "tile"), None),
        P(("grp", "tile")),
    )
    return jax.shard_map(
        functools.partial(body, mesh.shape["tile"]),
        mesh=mesh,
        in_specs=placed,
        out_specs=(P(("grp", "tile"), None, None), P(("grp", "mode"), None, None)),
        check_vma=False,
    )
```

```python
import functools

import jax
import jax.numpy as jnp
import numpy as np
from jax import lax
from jax.experimental import pallas as pl
from jax.experimental.pallas import tpu as pltpu
from jax.sharding import PartitionSpec as P

FRAME = 128
MIN_ROWS = 8


def dft_table():
    indices = np.arange(FRAME)
    phases = (indices[:, None] * indices[None, :] % FRAME) * (2.0 * np.pi / FRAME)
    cos_part = np.cos(phases) / np.sqrt(FRAME)
    sin_part = -np.sin(phases) / np.sqrt(FRAME)
    table = np.concatenate([cos_part, sin_part], 1)
    return table.astype(jnp.bfloat16).astype(np.float32)


def stages_of(tiles):
    bits = tiles.bit_length() - 1
    assert tiles == 1 << bits
    stages, at, rows = [], 0, FRAME
    while at < bits:
        radix = 2
        after = rows // radix if rows // radix >= MIN_ROWS else rows
        stages.append((at, radix, rows, after))
        rows = after
        at += 1
    return stages


def tree(values, join):
    while len(values) > 1:
        values = [join(values[i], values[i + 1]) for i in range(0, len(values), 2)]
    return values[0]


def kernel(
    tiles,
    stages,
    obj,
    probe_given,
    frames_given,
    offsets,
    counts,
    table_given,
    obj_out,
    probe_out,
    probe,
    frames,
    table,
    fwd,
    inv,
    load_sem,
    ext,
    power_probe,
    ext_split,
    illum,
    illum_in,
    patches,
    far,
    power,
    power_in,
    factor,
    grad,
    grad_in,
    gext,
    spill_in,
    acc,
    peaks,
    halo_sem,
    relay_sem,
    pp_sem,
    illum_sem,
    power_sem,
    grad_sem,
    spill_sem,
    upd_sem,
    *staged,
):
    n_st = len(stages)
    rs_in, pk_in = staged[:n_st], staged[n_st : 2 * n_st]
    rs_sem, ag_sem, pk_sem = (staged[(2 + j) * n_st : (3 + j) * n_st] for j in range(3))
    slots = frames.shape[0]
    modes = probe.shape[0]
    f = FRAME
    me = lax.axis_index("tile")
    core = lax.axis_index("mode")
    other = 1 - core
    has_left, has_right = me > 0, me < tiles - 1
    left, right = jnp.maximum(me - 1, 0), jnp.minimum(me + 1, tiles - 1)

    def remote(src, dst, sems, **where):
        return pltpu.make_async_remote_copy(
            src_ref=src,
            dst_ref=dst,
            send_sem=sems[0],
            recv_sem=sems[1],
            device_id=where,
            device_id_type=pl.DeviceIdType.MESH,
        )

    def pair(sem, *at):
        return (sem.at[(0, *at)], sem.at[(1, *at)])

    loads = [
        pltpu.make_async_copy(src, dst, load_sem.at[j])
        for j, (src, dst) in enumerate(
            [
                (probe_given, probe),
                (obj, ext.at[:, pl.ds(0, f)]),
                (table_given, table),
                (frames_given, frames),
            ]
        )
    ]
    for load in loads:
        load.start()

    barrier = pltpu.get_barrier_semaphore()

    def greet(**where):
        pl.semaphore_signal(
            barrier, inc=1, device_id=where, device_id_type=pl.DeviceIdType.MESH
        )

    greet(mode=other)
    greeted = 1
    for at, radix, _, _ in stages:
        for d in range(1, radix):
            greet(tile=me ^ (d << at))
            greeted += 1

    @pl.when(has_left)
    def _():
        greet(tile=left)

    @pl.when(has_right)
    def _():
        greet(tile=right)

    beside = jnp.minimum(me, 1) + jnp.minimum(tiles - 1 - me, 1)
    pl.semaphore_wait(barrier, greeted + beside)

    halo = remote(obj.at[core], ext.at[core, pl.ds(f, f)], pair(halo_sem), tile=left)

    @pl.when(has_left)
    def _():
        halo.start()

    loads[0].wait()
    own_power = jnp.zeros((f, f), jnp.float32)
    for k in range(modes):
        own_power += probe[k, :, :f] ** 2 + probe[k, :, f:] ** 2
    power_probe[0] = own_power
    pp_copy = remote(power_probe.at[0], power_probe.at[1], pair(pp_sem), mode=other)
    pp_copy.start()

    def each(step):
        for s in range(slots):
            step(s, 0)

    def live(s):
        return jnp.clip(counts[0] - s, 0, 1).astype(jnp.float32)

    def dot(a, b):
        return jnp.dot(a, b, preferred_element_type=jnp.float32)

    def split(x):
        high = x.astype(jnp.bfloat16)
        return high, (x - high.astype(jnp.float32)).astype(jnp.bfloat16)

    def shifts(rows, columns, by):
        i = lax.broadcasted_iota(jnp.int32, (rows, columns), 0)
        j = lax.broadcasted_iota(jnp.int32, (rows, columns), 1)
        apart = j - i if rows < columns else i - j
        return jnp.where(apart == by, 1.0, 0.0).astype(jnp.float32)

    def spread(s, values):
        across = shifts(f, 2 * f, offsets[1, s]).astype(jnp.bfloat16)
        down = (shifts(2 * f, f, offsets[0, s]) * live(s)).astype(jnp.bfloat16)
        wide = dot(jnp.concatenate(split(values), 0), across).astype(jnp.bfloat16)
        return dot(jnp.concatenate([down, down], 1), wide)

    pp_copy.wait()
    probe_power = power_probe[0] + power_probe[1]
    illum[...] = jnp.zeros_like(illum)

    def light(s, carry):
        illum[...] += spread(s, probe_power)
        return carry

    each(light)
    illum_copy = remote(illum.at[pl.ds(f, f)], illum_in, pair(illum_sem), tile=right)

    @pl.when(has_right)
    def _():
        illum_copy.start()

    relay = remote(
        ext.at[core, pl.ds(f, f)], ext.at[core, pl.ds(f, f)], pair(relay_sem), mode=other
    )

    @pl.when(has_right)
    def _():
        halo.wait_recv()
        relay.start()
        relay.wait_recv()

    @pl.when(jnp.logical_not(has_right))
    def _():
        ext[:, f:, :] = jnp.zeros((2, f, 2 * f), jnp.float32)

    loads[1].wait()
    for part in range(2):
        for j, piece in enumerate(split(ext[part])):
            ext_split[:, (2 * part + j) * 2 * f : (2 * part + j + 1) * 2 * f] = piece

    def window(s):
        down = (shifts(f, 2 * f, offsets[0, s]) * live(s)).astype(jnp.bfloat16)
        across = shifts(2 * f, f, offsets[1, s]).astype(jnp.bfloat16)
        rows = dot(down, ext_split[...]).astype(jnp.bfloat16)
        both = jnp.concatenate([rows[:, : 4 * f], rows[:, 4 * f :]], 0)
        return dot(both, jnp.concatenate([across, across], 0))

    def swap(x):
        return jnp.concatenate(
            [
                jnp.concatenate([x[:f, :f], x[f:, :f]], 1),
                jnp.concatenate([x[:f, f:], x[f:, f:]], 1),
            ],
            0,
        )

    def power_copy(s):
        return remote(power.at[s], power_in.at[s], pair(power_sem, s), mode=other)

    def forward(s, carry):
        patch = window(s)
        xr, xi = patch[:f], patch[f:]
        patches[s, :, :f] = xr
        patches[s, :, f:] = xi
        total = jnp.zeros((f, f), jnp.float32)
        for p in range(modes // 2):
            psi = []
            for k in (2 * p, 2 * p + 1):
                pr, pi = probe[k, :, :f], probe[k, :, f:]
                psi.append(
                    jnp.concatenate([pr * xr - pi * xi, pr * xi + pi * xr], 1).astype(jnp.bfloat16)
                )
            half = dot(jnp.concatenate(psi, 0), fwd[...]).astype(jnp.bfloat16)
            wave = dot(inv[...], swap(half))
            far[s, p] = wave
            squares = wave * wave
            total += (squares[:f, :f] + squares[f:, :f]) + (squares[:f, f:] + squares[f:, f:])
        power[s] = total
        power_copy(s).start()
        return carry

    loads[2].wait()
    for ref, sign in ((fwd, 1.0), (inv, -1.0)):
        ref[:f, :f] = table[:, :f].astype(jnp.bfloat16)
        ref[f:, f:] = table[:, :f].astype(jnp.bfloat16)
        ref[:f, f:] = (sign * table[:, f:]).astype(jnp.bfloat16)
        ref[f:, :f] = (-sign * table[:, f:]).astype(jnp.bfloat16)
    each(forward)

    @pl.when(has_left)
    def _():
        illum_copy.wait_recv()

    @pl.when(jnp.logical_not(has_left))
    def _():
        illum_in[...] = jnp.zeros_like(illum_in)

    @pl.when(has_right)
    def _():
        illum_copy.wait_send()

    illum[:f] = illum[:f] + illum_in[...]
    high = jnp.max(illum[:f].reshape(f // 8, 8, 2 * f), 0)
    peaks[0] = jnp.maximum(high[:, :f], high[:, f:])

    def peak_copies(i):
        at, radix, _, _ = stages[i]
        return [
            remote(
                peaks.at[i], pk_in[i].at[d - 1], pair(pk_sem[i], d - 1), tile=me ^ (d << at)
            )
            for d in range(1, radix)
        ]

    def peak_start(i):
        for copy in peak_copies(i):
            copy.start()

    def peak_finish(i):
        for copy in peak_copies(i):
            copy.wait()
        radix = stages[i][1]
        peaks[i + 1] = tree([peaks[i]] + [pk_in[i][d] for d in range(radix - 1)], jnp.maximum)

    peak_start(0)

    def rescale(s, carry):
        power_copy(s).wait()
        factor[s] = (
            jnp.sqrt(frames[s]) * lax.rsqrt(power[s] + power_in[s] + 1.0) - 1.0
        )
        return carry

    loads[3].wait()
    each(rescale)

    starts = [0]
    for at, radix, rows, after in stages:
        digit = lax.rem(me // (1 << at), radix)
        starts.append(starts[-1] + digit * after if after < rows else starts[-1])

    def rows_at(ref, k, start, rows):
        return ref.at[k, pl.ds(pl.multiple_of(start, MIN_ROWS), rows)]

    def rs_copies(i, k):
        at, radix, rows, after = stages[i]
        digit = lax.rem(me // (1 << at), radix)
        copies = []
        for d in range(1, radix):
            start = starts[i] + (digit ^ d) * after if after < rows else starts[i]
            copies.append(
                remote(
                    rows_at(acc, k, start, after),
                    rs_in[i].at[k, d - 1],
                    pair(rs_sem[i], k, d - 1),
                    tile=me ^ (d << at),
                )
            )
        return copies

    def rs_start(i, ks):
        for k in ks:
            for copy in rs_copies(i, k):
                copy.start()

    def rs_finish(i, ks):
        after, radix = stages[i][3], stages[i][1]
        for k in ks:
            for copy in rs_copies(i, k):
                copy.wait()
            here = rows_at(acc, k, starts[i + 1], after)
            here[...] = tree(
                [here[...]] + [rs_in[i][k, d] for d in range(radix - 1)], lax.add
            )

    scale = 1.0 / np.sqrt(np.float32(tiles * slots))

    def finish_sum(ks):
        for k in ks:
            last = stages[-1][3]
            rows_at(probe_out, k, starts[-1], last)[...] = (
                rows_at(acc, k, starts[-1], last)[...] * scale
            )

    def ag_copies(i, k):
        at, radix, rows, after = stages[i]
        if after == rows:
            return []
        here = rows_at(probe_out, k, starts[i + 1], after)
        return [
            remote(here, here, pair(ag_sem[i], k, d - 1), tile=me ^ (d << at))
            for d in range(1, radix)
        ]

    def ag_start(i, ks):
        for k in ks:
            for copy in ag_copies(i, k):
                copy.start()

    def ag_finish(i, ks):
        for k in ks:
            for copy in ag_copies(i, k):
                copy.wait()

    groups = [(2 * p, 2 * p + 1) for p in range(modes // 2)]
    for p, ks in enumerate(groups):
        for k in ks:
            acc[k] = jnp.zeros((f, 2 * f), jnp.float32)

        def backward(s, carry, p=p, ks=ks):
            scaled = factor[s]
            wide = jnp.concatenate([scaled, scaled], 1)
            wide = jnp.concatenate([wide, wide], 0)
            corrected = (far[s, p] * wide).astype(jnp.bfloat16)
            half = dot(swap(corrected), inv[...]).astype(jnp.bfloat16)
            back = dot(fwd[...], swap(half))
            xr, xi = patches[s, :, :f], patches[s, :, f:]
            gr, gi = None, None
            for j, k in enumerate(ks):
                br, bi = back[:f, j * f : (j + 1) * f], back[f:, j * f : (j + 1) * f]
                pr, pi = probe[k, :, :f], probe[k, :, f:]
                r, i = pr * br + pi * bi, pr * bi - pi * br
                gr, gi = (r, i) if gr is None else (gr + r, gi + i)
                acc[k, :, :f] += xr * br + xi * bi
                acc[k, :, f:] += xr * bi - xi * br
            if p == 0:
                grad[0, s], grad[1, s] = gr, gi
            else:
                grad[0, s] += gr
                grad[1, s] += gi
            return carry

        each(backward)
        if p == len(groups) - 1:
            grad_copy = remote(grad.at[other], grad_in, pair(grad_sem), mode=other)
            grad_copy.start()
        rs_start(0, ks)
        if p < n_st:
            peak_finish(p)
            if p + 1 < n_st:
                peak_start(p + 1)

    for i in range(len(groups), n_st):
        peak_finish(i)
        if i + 1 < n_st:
            peak_start(i + 1)

    def advance(i, k):
        rs_finish(i, (k,))
        if i + 1 < n_st:
            rs_start(i + 1, (k,))
        else:
            finish_sum((k,))
            ag_start(i, (k,))

    early = groups[0]
    for k in early:
        advance(0, k)

    grad_copy.wait()
    gext[...] = jnp.zeros_like(gext)

    def gather_up(s, carry):
        gext[...] += spread(s, grad[core, s] + grad_in[s])
        return carry

    each(gather_up)
    spill_copy = remote(gext.at[pl.ds(f, f)], spill_in, pair(spill_sem), tile=right)

    @pl.when(has_right)
    def _():
        spill_copy.start()

    for i in range(n_st):
        for k in range(modes):
            if i > 0 or k not in early:
                advance(i, k)

    @pl.when(has_left)
    def _():
        spill_copy.wait_recv()

    @pl.when(jnp.logical_not(has_left))
    def _():
        spill_in[...] = jnp.zeros_like(spill_in)

    peak = jnp.max(peaks[n_st])
    obj_out[core] = ext[core, :f] + (gext[:f] + spill_in[...]) / (illum[:f] + 0.1 * peak)
    upd_copy = remote(obj_out.at[core], obj_out.at[core], pair(upd_sem), mode=other)
    upd_copy.start()

    for i in reversed(range(n_st)):
        for k in range(modes):
            ag_finish(i, (k,))
            if i > 0:
                ag_start(i - 1, (k,))

    upd_copy.wait()

    @pl.when(has_left)
    def _():
        halo.wait_send()

    @pl.when(has_right)
    def _():
        relay.wait_send()
        spill_copy.wait_send()


def body(tiles, object_slab, probe_modes, frames, offsets, counts):
    f = FRAME
    stages = stages_of(tiles)
    slots, modes = frames.shape[0], probe_modes.shape[0]
    columns = object_slab.shape[2]
    table = dft_table()
    f32 = jnp.float32
    vmem = pl.BlockSpec(memory_space=pltpu.VMEM)
    hbm = pl.BlockSpec(memory_space=pltpu.HBM)
    smem = pl.BlockSpec(memory_space=pltpu.SMEM)
    dma = pltpu.SemaphoreType.DMA
    scratch = [
        pltpu.VMEM(probe_modes.shape, f32),
        pltpu.VMEM(frames.shape, f32),
        pltpu.VMEM(table.shape, f32),
        pltpu.VMEM((2 * f, 2 * f), jnp.bfloat16),
        pltpu.VMEM((2 * f, 2 * f), jnp.bfloat16),
        dma((4,)),
        pltpu.VMEM((2, 2 * f, columns), f32),
        pltpu.VMEM((2, f, f), f32),
        pltpu.VMEM((2 * f, 4 * columns), jnp.bfloat16),
        pltpu.VMEM((2 * f, columns), f32),
        pltpu.VMEM((f, columns), f32),
        pltpu.VMEM((slots, f, 2 * f), f32),
        pltpu.VMEM((slots, modes // 2, 2 * f, 2 * f), f32),
        pltpu.VMEM((slots, f, f), f32),
        pltpu.VMEM((slots, f, f), f32),
        pltpu.VMEM((slots, f, f), f32),
        pltpu.VMEM((2, slots, f, f), f32),
        pltpu.VMEM((slots, f, f), f32),
        pltpu.VMEM((2 * f, columns), f32),
        pltpu.VMEM((f, columns), f32),
        pltpu.VMEM((modes, f, 2 * f), f32),
        pltpu.VMEM((len(stages) + 1, 8, f), f32),
        dma((2,)),
        dma((2,)),
        dma((2,)),
        dma((2,)),
        dma((2, slots)),
        dma((2,)),
        dma((2,)),
        dma((2,)),
    ]
    scratch += [pltpu.VMEM((modes, radix - 1, after, 2 * f), f32) for _, radix, _, after in stages]
    scratch += [pltpu.VMEM((radix - 1, 8, f), f32) for _, radix, _, _ in stages]
    for _ in range(2):
        scratch += [dma((2, modes, radix - 1)) for _, radix, _, _ in stages]
    scratch += [dma((2, radix - 1)) for _, radix, _, _ in stages]
    updated, probe_direction = pl.pallas_call(
        functools.partial(kernel, tiles, stages),
        out_shape=(
            jax.ShapeDtypeStruct((2, f, columns), f32),
            jax.ShapeDtypeStruct((modes, f, 2 * f), f32),
        ),
        in_specs=[hbm, hbm, hbm, smem, smem, hbm],
        out_specs=(vmem, vmem),
        scratch_shapes=scratch,
        compiler_params=pltpu.CompilerParams(
            collective_id=0, has_side_effects=True, vmem_limit_bytes=60 * 1024 * 1024
        ),
        name="ptycho_step",
    )(object_slab.transpose(1, 0, 2), probe_modes, frames, offsets.T, counts, table)
    return updated.transpose(1, 0, 2), probe_direction


def solution(mesh):
    placed = (
        P(("grp", "tile"), None, None),
        P(("grp", "mode"), None, None),
        P(("grp", "tile"), None, None),
        P(("grp", "tile"), None),
        P(("grp", "tile")),
    )
    return jax.shard_map(
        functools.partial(body, mesh.shape["tile"]),
        mesh=mesh,
        in_specs=placed,
        out_specs=(P(("grp", "tile"), None, None), P(("grp", "mode"), None, None)),
        check_vma=False,
    )
```

```python
import functools

import jax
import jax.numpy as jnp
import numpy as np
from jax import lax
from jax.experimental import pallas as pl
from jax.experimental.pallas import tpu as pltpu
from jax.sharding import PartitionSpec as P

FRAME = 128
MIN_ROWS = 8


def dft_table():
    indices = np.arange(FRAME)
    phases = (indices[:, None] * indices[None, :] % FRAME) * (2.0 * np.pi / FRAME)
    cos_part = np.cos(phases) / np.sqrt(FRAME)
    sin_part = -np.sin(phases) / np.sqrt(FRAME)
    table = np.concatenate([cos_part, sin_part], 1)
    return table.astype(jnp.bfloat16).astype(np.float32)


def stages_of(tiles):
    bits = tiles.bit_length() - 1
    assert tiles == 1 << bits
    stages, at, rows = [], 0, FRAME
    while at < bits:
        radix = 2 if at == 0 or bits - at == 1 else 4
        after = rows // radix if rows // radix >= MIN_ROWS else rows
        stages.append((at, radix, rows, after))
        rows = after
        at += 1 if radix == 2 else 2
    return stages


def tree(values, join):
    while len(values) > 1:
        values = [join(values[i], values[i + 1]) for i in range(0, len(values), 2)]
    return values[0]


def kernel(
    tiles,
    stages,
    obj,
    probe_given,
    frames_given,
    offsets,
    counts,
    table_given,
    obj_out,
    probe_out,
    probe,
    frames,
    table,
    fwd,
    inv,
    load_sem,
    ext,
    power_probe,
    ext_split,
    illum,
    illum_in,
    patches,
    far,
    power,
    power_in,
    factor,
    grad,
    grad_in,
    gext,
    spill_in,
    acc,
    peaks,
    halo_sem,
    relay_sem,
    pp_sem,
    illum_sem,
    power_sem,
    grad_sem,
    spill_sem,
    upd_sem,
    *staged,
):
    n_st = len(stages)
    rs_in, pk_in = staged[:n_st], staged[n_st : 2 * n_st]
    rs_sem, ag_sem, pk_sem = (staged[(2 + j) * n_st : (3 + j) * n_st] for j in range(3))
    slots = frames.shape[0]
    modes = probe.shape[0]
    f = FRAME
    me = lax.axis_index("tile")
    core = lax.axis_index("mode")
    other = 1 - core
    has_left, has_right = me > 0, me < tiles - 1
    left, right = jnp.maximum(me - 1, 0), jnp.minimum(me + 1, tiles - 1)

    def remote(src, dst, sems, **where):
        return pltpu.make_async_remote_copy(
            src_ref=src,
            dst_ref=dst,
            send_sem=sems[0],
            recv_sem=sems[1],
            device_id=where,
            device_id_type=pl.DeviceIdType.MESH,
        )

    def pair(sem, *at):
        return (sem.at[(0, *at)], sem.at[(1, *at)])

    loads = [
        pltpu.make_async_copy(src, dst, load_sem.at[j])
        for j, (src, dst) in enumerate(
            [
                (probe_given, probe),
                (obj, ext.at[:, pl.ds(0, f)]),
                (table_given, table),
                (frames_given, frames),
            ]
        )
    ]
    for load in loads:
        load.start()

    barrier = pltpu.get_barrier_semaphore()

    def greet(**where):
        pl.semaphore_signal(
            barrier, inc=1, device_id=where, device_id_type=pl.DeviceIdType.MESH
        )

    greet(mode=other)
    greeted = 1
    for at, radix, _, _ in stages:
        for d in range(1, radix):
            greet(tile=me ^ (d << at))
            greeted += 1

    @pl.when(has_left)
    def _():
        greet(tile=left)

    @pl.when(has_right)
    def _():
        greet(tile=right)

    beside = jnp.minimum(me, 1) + jnp.minimum(tiles - 1 - me, 1)
    pl.semaphore_wait(barrier, greeted + beside)

    halo = remote(obj.at[core], ext.at[core, pl.ds(f, f)], pair(halo_sem), tile=left)

    @pl.when(has_left)
    def _():
        halo.start()

    loads[0].wait()
    own_power = jnp.zeros((f, f), jnp.float32)
    for k in range(modes):
        own_power += probe[k, :, :f] ** 2 + probe[k, :, f:] ** 2
    power_probe[0] = own_power
    pp_copy = remote(power_probe.at[0], power_probe.at[1], pair(pp_sem), mode=other)
    pp_copy.start()

    def each(step):
        lax.fori_loop(0, slots, step, 0)

    def live(s):
        return jnp.clip(counts[0] - s, 0, 1).astype(jnp.float32)

    def dot(a, b):
        return jnp.dot(a, b, preferred_element_type=jnp.float32)

    def split(x):
        high = x.astype(jnp.bfloat16)
        return high, (x - high.astype(jnp.float32)).astype(jnp.bfloat16)

    def shifts(rows, columns, by):
        i = lax.broadcasted_iota(jnp.int32, (rows, columns), 0)
        j = lax.broadcasted_iota(jnp.int32, (rows, columns), 1)
        apart = j - i if rows < columns else i - j
        return jnp.where(apart == by, 1.0, 0.0).astype(jnp.float32)

    def spread(s, values):
        across = shifts(f, 2 * f, offsets[1, s]).astype(jnp.bfloat16)
        down = (shifts(2 * f, f, offsets[0, s]) * live(s)).astype(jnp.bfloat16)
        wide = dot(jnp.concatenate(split(values), 0), across).astype(jnp.bfloat16)
        return dot(jnp.concatenate([down, down], 1), wide)

    pp_copy.wait()
    probe_power = power_probe[0] + power_probe[1]
    illum[...] = jnp.zeros_like(illum)

    def light(s, carry):
        illum[...] += spread(s, probe_power)
        return carry

    each(light)
    illum_copy = remote(illum.at[pl.ds(f, f)], illum_in, pair(illum_sem), tile=right)

    @pl.when(has_right)
    def _():
        illum_copy.start()

    relay = remote(
        ext.at[core, pl.ds(f, f)], ext.at[core, pl.ds(f, f)], pair(relay_sem), mode=other
    )

    @pl.when(has_right)
    def _():
        halo.wait_recv()
        relay.start()
        relay.wait_recv()

    @pl.when(jnp.logical_not(has_right))
    def _():
        ext[:, f:, :] = jnp.zeros((2, f, 2 * f), jnp.float32)

    loads[1].wait()
    for part in range(2):
        for j, piece in enumerate(split(ext[part])):
            ext_split[:, (2 * part + j) * 2 * f : (2 * part + j + 1) * 2 * f] = piece

    def window(s):
        down = (shifts(f, 2 * f, offsets[0, s]) * live(s)).astype(jnp.bfloat16)
        across = shifts(2 * f, f, offsets[1, s]).astype(jnp.bfloat16)
        rows = dot(down, ext_split[...]).astype(jnp.bfloat16)
        both = jnp.concatenate([rows[:, : 4 * f], rows[:, 4 * f :]], 0)
        return dot(both, jnp.concatenate([across, across], 0))

    def swap(x):
        return jnp.concatenate(
            [
                jnp.concatenate([x[:f, :f], x[f:, :f]], 1),
                jnp.concatenate([x[:f, f:], x[f:, f:]], 1),
            ],
            0,
        )

    def power_copy(s):
        return remote(power.at[s], power_in.at[s], pair(power_sem, s), mode=other)

    def forward(s, carry):
        patch = window(s)
        xr, xi = patch[:f], patch[f:]
        patches[s, :, :f] = xr
        patches[s, :, f:] = xi
        total = jnp.zeros((f, f), jnp.float32)
        for p in range(modes // 2):
            psi = []
            for k in (2 * p, 2 * p + 1):
                pr, pi = probe[k, :, :f], probe[k, :, f:]
                psi.append(
                    jnp.concatenate([pr * xr - pi * xi, pr * xi + pi * xr], 1).astype(jnp.bfloat16)
                )
            half = dot(jnp.concatenate(psi, 0), fwd[...]).astype(jnp.bfloat16)
            wave = dot(inv[...], swap(half))
            far[s, p] = wave
            squares = wave * wave
            total += (squares[:f, :f] + squares[f:, :f]) + (squares[:f, f:] + squares[f:, f:])
        power[s] = total
        power_copy(s).start()
        return carry

    loads[2].wait()
    for ref, sign in ((fwd, 1.0), (inv, -1.0)):
        ref[:f, :f] = table[:, :f].astype(jnp.bfloat16)
        ref[f:, f:] = table[:, :f].astype(jnp.bfloat16)
        ref[:f, f:] = (sign * table[:, f:]).astype(jnp.bfloat16)
        ref[f:, :f] = (-sign * table[:, f:]).astype(jnp.bfloat16)
    each(forward)

    @pl.when(has_left)
    def _():
        illum_copy.wait_recv()

    @pl.when(jnp.logical_not(has_left))
    def _():
        illum_in[...] = jnp.zeros_like(illum_in)

    @pl.when(has_right)
    def _():
        illum_copy.wait_send()

    illum[:f] = illum[:f] + illum_in[...]
    high = jnp.max(illum[:f].reshape(f // 8, 8, 2 * f), 0)
    peaks[0] = jnp.maximum(high[:, :f], high[:, f:])

    def peak_copies(i):
        at, radix, _, _ = stages[i]
        return [
            remote(
                peaks.at[i], pk_in[i].at[d - 1], pair(pk_sem[i], d - 1), tile=me ^ (d << at)
            )
            for d in range(1, radix)
        ]

    def peak_start(i):
        for copy in peak_copies(i):
            copy.start()

    def peak_finish(i):
        for copy in peak_copies(i):
            copy.wait()
        radix = stages[i][1]
        peaks[i + 1] = tree([peaks[i]] + [pk_in[i][d] for d in range(radix - 1)], jnp.maximum)

    peak_start(0)

    def rescale(s, carry):
        power_copy(s).wait()
        factor[s] = (
            jnp.sqrt(frames[s]) * lax.rsqrt(power[s] + power_in[s] + 1.0) - 1.0
        )
        return carry

    loads[3].wait()
    each(rescale)

    starts = [0]
    for at, radix, rows, after in stages:
        digit = lax.rem(me // (1 << at), radix)
        starts.append(starts[-1] + digit * after if after < rows else starts[-1])

    def rows_at(ref, k, start, rows):
        return ref.at[k, pl.ds(pl.multiple_of(start, MIN_ROWS), rows)]

    def rs_copies(i, k):
        at, radix, rows, after = stages[i]
        digit = lax.rem(me // (1 << at), radix)
        copies = []
        for d in range(1, radix):
            start = starts[i] + (digit ^ d) * after if after < rows else starts[i]
            copies.append(
                remote(
                    rows_at(acc, k, start, after),
                    rs_in[i].at[k, d - 1],
                    pair(rs_sem[i], k, d - 1),
                    tile=me ^ (d << at),
                )
            )
        return copies

    def rs_start(i, ks):
        for k in ks:
            for copy in rs_copies(i, k):
                copy.start()

    def rs_finish(i, ks):
        after, radix = stages[i][3], stages[i][1]
        for k in ks:
            for copy in rs_copies(i, k):
                copy.wait()
            here = rows_at(acc, k, starts[i + 1], after)
            here[...] = tree(
                [here[...]] + [rs_in[i][k, d] for d in range(radix - 1)], lax.add
            )

    scale = 1.0 / np.sqrt(np.float32(tiles * slots))

    def finish_sum(ks):
        for k in ks:
            last = stages[-1][3]
            rows_at(probe_out, k, starts[-1], last)[...] = (
                rows_at(acc, k, starts[-1], last)[...] * scale
            )

    def ag_copies(i, k):
        at, radix, rows, after = stages[i]
        if after == rows:
            return []
        here = rows_at(probe_out, k, starts[i + 1], after)
        return [
            remote(here, here, pair(ag_sem[i], k, d - 1), tile=me ^ (d << at))
            for d in range(1, radix)
        ]

    def ag_start(i, ks):
        for k in ks:
            for copy in ag_copies(i, k):
                copy.start()

    def ag_finish(i, ks):
        for k in ks:
            for copy in ag_copies(i, k):
                copy.wait()

    groups = [(2 * p, 2 * p + 1) for p in range(modes // 2)]
    for p, ks in enumerate(groups):
        for k in ks:
            acc[k] = jnp.zeros((f, 2 * f), jnp.float32)

        def backward(s, carry, p=p, ks=ks):
            scaled = factor[s]
            wide = jnp.concatenate([scaled, scaled], 1)
            wide = jnp.concatenate([wide, wide], 0)
            corrected = (far[s, p] * wide).astype(jnp.bfloat16)
            half = dot(swap(corrected), inv[...]).astype(jnp.bfloat16)
            back = dot(fwd[...], swap(half))
            xr, xi = patches[s, :, :f], patches[s, :, f:]
            gr, gi = None, None
            for j, k in enumerate(ks):
                br, bi = back[:f, j * f : (j + 1) * f], back[f:, j * f : (j + 1) * f]
                pr, pi = probe[k, :, :f], probe[k, :, f:]
                r, i = pr * br + pi * bi, pr * bi - pi * br
                gr, gi = (r, i) if gr is None else (gr + r, gi + i)
                acc[k, :, :f] += xr * br + xi * bi
                acc[k, :, f:] += xr * bi - xi * br
            if p == 0:
                grad[0, s], grad[1, s] = gr, gi
            else:
                grad[0, s] += gr
                grad[1, s] += gi
            return carry

        each(backward)
        if p == len(groups) - 1:
            grad_copy = remote(grad.at[other], grad_in, pair(grad_sem), mode=other)
            grad_copy.start()
        rs_start(0, ks)
        if p < n_st:
            peak_finish(p)
            if p + 1 < n_st:
                peak_start(p + 1)

    for i in range(len(groups), n_st):
        peak_finish(i)
        if i + 1 < n_st:
            peak_start(i + 1)

    def advance(i, k):
        rs_finish(i, (k,))
        if i + 1 < n_st:
            rs_start(i + 1, (k,))
        else:
            finish_sum((k,))
            ag_start(i, (k,))

    early = groups[0]
    for k in early:
        advance(0, k)

    grad_copy.wait()
    gext[...] = jnp.zeros_like(gext)

    def gather_up(s, carry):
        gext[...] += spread(s, grad[core, s] + grad_in[s])
        return carry

    each(gather_up)
    spill_copy = remote(gext.at[pl.ds(f, f)], spill_in, pair(spill_sem), tile=right)

    @pl.when(has_right)
    def _():
        spill_copy.start()

    for i in range(n_st):
        for k in range(modes):
            if i > 0 or k not in early:
                advance(i, k)

    @pl.when(has_left)
    def _():
        spill_copy.wait_recv()

    @pl.when(jnp.logical_not(has_left))
    def _():
        spill_in[...] = jnp.zeros_like(spill_in)

    peak = jnp.max(peaks[n_st])
    obj_out[core] = ext[core, :f] + (gext[:f] + spill_in[...]) / (illum[:f] + 0.1 * peak)
    upd_copy = remote(obj_out.at[core], obj_out.at[core], pair(upd_sem), mode=other)
    upd_copy.start()

    for i in reversed(range(n_st)):
        for k in range(modes):
            ag_finish(i, (k,))
            if i > 0:
                ag_start(i - 1, (k,))

    upd_copy.wait()

    @pl.when(has_left)
    def _():
        halo.wait_send()

    @pl.when(has_right)
    def _():
        relay.wait_send()
        spill_copy.wait_send()


def body(tiles, object_slab, probe_modes, frames, offsets, counts):
    f = FRAME
    stages = stages_of(tiles)
    slots, modes = frames.shape[0], probe_modes.shape[0]
    columns = object_slab.shape[2]
    table = dft_table()
    f32 = jnp.float32
    vmem = pl.BlockSpec(memory_space=pltpu.VMEM)
    hbm = pl.BlockSpec(memory_space=pltpu.HBM)
    smem = pl.BlockSpec(memory_space=pltpu.SMEM)
    dma = pltpu.SemaphoreType.DMA
    scratch = [
        pltpu.VMEM(probe_modes.shape, f32),
        pltpu.VMEM(frames.shape, f32),
        pltpu.VMEM(table.shape, f32),
        pltpu.VMEM((2 * f, 2 * f), jnp.bfloat16),
        pltpu.VMEM((2 * f, 2 * f), jnp.bfloat16),
        dma((4,)),
        pltpu.VMEM((2, 2 * f, columns), f32),
        pltpu.VMEM((2, f, f), f32),
        pltpu.VMEM((2 * f, 4 * columns), jnp.bfloat16),
        pltpu.VMEM((2 * f, columns), f32),
        pltpu.VMEM((f, columns), f32),
        pltpu.VMEM((slots, f, 2 * f), f32),
        pltpu.VMEM((slots, modes // 2, 2 * f, 2 * f), f32),
        pltpu.VMEM((slots, f, f), f32),
        pltpu.VMEM((slots, f, f), f32),
        pltpu.VMEM((slots, f, f), f32),
        pltpu.VMEM((2, slots, f, f), f32),
        pltpu.VMEM((slots, f, f), f32),
        pltpu.VMEM((2 * f, columns), f32),
        pltpu.VMEM((f, columns), f32),
        pltpu.VMEM((modes, f, 2 * f), f32),
        pltpu.VMEM((len(stages) + 1, 8, f), f32),
        dma((2,)),
        dma((2,)),
        dma((2,)),
        dma((2,)),
        dma((2, slots)),
        dma((2,)),
        dma((2,)),
        dma((2,)),
    ]
    scratch += [pltpu.VMEM((modes, radix - 1, after, 2 * f), f32) for _, radix, _, after in stages]
    scratch += [pltpu.VMEM((radix - 1, 8, f), f32) for _, radix, _, _ in stages]
    for _ in range(2):
        scratch += [dma((2, modes, radix - 1)) for _, radix, _, _ in stages]
    scratch += [dma((2, radix - 1)) for _, radix, _, _ in stages]
    updated, probe_direction = pl.pallas_call(
        functools.partial(kernel, tiles, stages),
        out_shape=(
            jax.ShapeDtypeStruct((2, f, columns), f32),
            jax.ShapeDtypeStruct((modes, f, 2 * f), f32),
        ),
        in_specs=[hbm, hbm, hbm, smem, smem, hbm],
        out_specs=(vmem, vmem),
        scratch_shapes=scratch,
        compiler_params=pltpu.CompilerParams(
            collective_id=0, has_side_effects=True, vmem_limit_bytes=60 * 1024 * 1024
        ),
        name="ptycho_step",
    )(object_slab.transpose(1, 0, 2), probe_modes, frames, offsets.T, counts, table)
    return updated.transpose(1, 0, 2), probe_direction


def solution(mesh):
    placed = (
        P(("grp", "tile"), None, None),
        P(("grp", "mode"), None, None),
        P(("grp", "tile"), None, None),
        P(("grp", "tile"), None),
        P(("grp", "tile")),
    )
    return jax.shard_map(
        functools.partial(body, mesh.shape["tile"]),
        mesh=mesh,
        in_specs=placed,
        out_specs=(P(("grp", "tile"), None, None), P(("grp", "mode"), None, None)),
        check_vma=False,
    )
```
